256 devices in a mesh: pb: 8 (over x, y_lo), pa: 32 (over y_hi, z, core).
Axes of the slice: x: 4, y: 4 (y_hi: 2, y_lo: 2; y = y_hi * 2 + y_lo), z: 8, core: 2. Of those that a mesh axis runs over, the one named last changes fastest.
Arguments:
- questions: bfloat16 [16384, 4096], P(('pb', 'pa')), may hold values from -1 to 1
- passages: bfloat16 [16384, 4096], P(('pa', 'pb')), may hold values from -1 to 1
- hard_rows: bfloat16 [16384, 4096], P(('pa', 'pb')), may hold values from -1 to 1
- hard_index: int32 [16384], P('pb'), may hold values from 0 to 16383, as said below
- projection: bfloat16 [4096, 768], replicated, may hold values from -0.09375 to 0.09375
Outputs:
- grad_questions: bfloat16 [16384, 4096], P(('pb', 'pa'))
- grad_passages: bfloat16 [16384, 4096], P(('pa', 'pb'))
- grad_hard: bfloat16 [16384, 4096], P(('pa', 'pb'))
- question_loss: float32 [16384], P(('pb', 'pa'))
- passage_loss: float32 [16384], P(('pa', 'pb'))
The draws below stay inside these ranges and needn't reach their ends.
Inputs may be any that keep to these rules, and one draw needn't show every extreme that they name: `hard_index`: the rows come in aligned blocks of 512 questions; the hard negative of a question lies in the same aligned block of 512 rows of hard_rows, and within a block every hard row is named by exactly one question.
All inputs are finite; a program needn't handle non-finite values.
Results may differ from the reference program's by a relative error of at most 0.024.
Values may be sent and summed in bfloat16 or wider, within the bound.
A program may use at most 128 MiB of HBM per device.

```python
import math
import jax
import jax.numpy as jnp
from jax import lax

D_MODEL = 4096
D_EMB = 768
BATCH = 16384
QBLOCK = 2048
PBLOCK = 512
N_PB = 8
N_PA = 32


def shared_rows(key):
    return jnp.clip(jax.random.normal(key, (BATCH, D_MODEL), jnp.float32), -4.0, 4.0)


def block_order(key):
    key = jax.random.fold_in(key, 71)
    block_count = BATCH // PBLOCK
    rank_keys = jax.random.randint(key, (block_count, PBLOCK), 0, 1 << 20) * PBLOCK
    rank_keys = rank_keys + jnp.arange(PBLOCK, dtype=jnp.int32)[None, :]
    return jnp.argsort(rank_keys, axis=1, stable=True).astype(jnp.int32)


def mix_rows(common_rows, own_noise, row_scale, common_weight, own_weight):
    return (row_scale * (common_weight * common_rows + own_weight * own_noise)).astype(jnp.bfloat16)


def draw_questions(key, part):
    common_rows = shared_rows(key)
    key = jax.random.fold_in(key, 1)
    noise_key = jax.random.fold_in(key, 0)
    own_noise = jnp.clip(jax.random.normal(noise_key, (BATCH, D_MODEL), jnp.float32), -4.0, 4.0)
    row_scale = 0.05
    return mix_rows(common_rows, own_noise, row_scale, 0.5, 0.85)


def draw_passages(key, part):
    common_rows = shared_rows(key)
    key = jax.random.fold_in(key, 2)
    noise_key = jax.random.fold_in(key, 0)
    own_noise = jnp.clip(jax.random.normal(noise_key, (BATCH, D_MODEL), jnp.float32), -4.0, 4.0)
    row_scale = 0.05
    return mix_rows(common_rows, own_noise, row_scale, 0.5, 0.85)


def draw_hard_rows(key, part):
    common_rows = shared_rows(key).reshape(BATCH // PBLOCK, PBLOCK, D_MODEL)
    inverse = jnp.argsort(block_order(key), axis=1, stable=True)
    mapped = jnp.take_along_axis(common_rows, inverse[:, :, None], axis=1).reshape(BATCH, D_MODEL)
    key = jax.random.fold_in(key, 3)
    noise_key = jax.random.fold_in(key, 0)
    own_noise = jnp.clip(jax.random.normal(noise_key, (BATCH, D_MODEL), jnp.float32), -4.0, 4.0)
    row_scale = 0.05
    return mix_rows(mapped, own_noise, row_scale, 0.45, 0.89)


def draw_hard_index(key, part):
    block_perm = block_order(key)
    block_base = jnp.arange(BATCH // PBLOCK, dtype=jnp.int32) * PBLOCK
    return (block_perm + block_base[:, None]).reshape(BATCH)


def centred(rng, shape, width, bound, held_as=jnp.bfloat16):
    return jnp.clip(width * jax.random.normal(rng, shape, jnp.float32), -bound, bound).astype(held_as)


def setup_inputs(seed: int = 0) -> dict:
    keys = jax.random.split(jax.random.key(seed), 6)
    questions = draw_questions(jax.random.fold_in(keys[5], 71), 0)
    passages = draw_passages(jax.random.fold_in(keys[5], 71), 0)
    hard_rows = draw_hard_rows(jax.random.fold_in(keys[5], 71), 0)
    hard_index = draw_hard_index(jax.random.fold_in(keys[5], 71), 0)
    projection = centred(keys[4], (D_MODEL, D_EMB), D_MODEL ** -0.5, 0.09375)
    return dict(questions=questions, passages=passages, hard_rows=hard_rows, hard_index=hard_index, projection=projection)


inverse_temp = 40.0
epsilon = 1e-06

def project_rows(pooled, projection):
    embedded = jnp.dot(pooled, projection, preferred_element_type=jnp.float32)
    inv_norm = lax.rsqrt(lax.optimization_barrier(jnp.sum(embedded * embedded, axis=1, keepdims=True)) + epsilon)
    return (embedded * inv_norm, inv_norm)

def unit_grad(grad_unit, unit_rows, inv_norm):
    along_unit = lax.optimization_barrier(jnp.sum(grad_unit * unit_rows, axis=1, keepdims=True))
    return ((grad_unit - unit_rows * along_unit) * inv_norm).astype(jnp.bfloat16)

def round_low(values):
    return lax.optimization_barrier(values.astype(jnp.bfloat16)).astype(jnp.float32)

def reference(questions, passages, hard_rows, hard_index, projection):
    q_unit, q_norm = project_rows(questions, projection)
    p_unit, p_norm = project_rows(passages, projection)
    h_unit, h_norm = project_rows(hard_rows, projection)
    q_low = q_unit.astype(jnp.bfloat16)
    p_low = p_unit.astype(jnp.bfloat16)
    h_low = h_unit.astype(jnp.bfloat16)
    hard_picked = jnp.take(h_low, hard_index, axis=0)
    hard_score = inverse_temp * lax.optimization_barrier(jnp.sum(q_low.astype(jnp.float32) * hard_picked.astype(jnp.float32), axis=1))
    hard_exp = jnp.exp(hard_score - inverse_temp)
    block_rows = math.gcd(QBLOCK, 512)
    block_count = BATCH // block_rows
    per_group = QBLOCK // block_rows
    column_ids = jnp.arange(BATCH, dtype=jnp.int32)
    p_flip = p_low.T
    p_blocks = p_low.astype(jnp.float32).reshape(N_PA, PBLOCK, D_EMB)
    block_names = jnp.arange(N_PA, dtype=jnp.int32)

    def score_block(block_index):
        first_row = (block_index * block_rows).astype(jnp.int32)
        query_part = lax.dynamic_slice_in_dim(q_low, first_row, block_rows, 0)
        score_tile = inverse_temp * jnp.dot(query_part, p_flip, preferred_element_type=jnp.float32)
        row_ids = first_row + jnp.arange(block_rows, dtype=jnp.int32)
        diagonal = row_ids[:, None] == column_ids[None, :]
        return (first_row, row_ids, query_part, score_tile, diagonal)

    def forward_pass(column_sum, block_index):
        first_row, row_ids, query_part, score_tile, diagonal = score_block(block_index)
        exp_tile = jnp.exp(score_tile - inverse_temp)
        row_sum = lax.optimization_barrier(jnp.sum(exp_tile, axis=1)) + lax.dynamic_slice_in_dim(hard_exp, first_row, block_rows, 0)
        diag_score = lax.optimization_barrier(jnp.sum(jnp.where(diagonal, score_tile, 0.0), axis=1))
        return (column_sum + lax.optimization_barrier(jnp.sum(exp_tile, axis=0)), (row_sum, diag_score))
    block_ids = jnp.arange(block_count, dtype=jnp.int32)
    column_total, (row_total, diag_score) = lax.scan(forward_pass, jnp.zeros((BATCH,), jnp.float32), block_ids)
    row_total = row_total.reshape(BATCH)
    diag_score = diag_score.reshape(BATCH)
    question_loss = inverse_temp + jnp.log(row_total) - diag_score
    passage_loss = inverse_temp + jnp.log(column_total) - diag_score
    hard_weight = hard_exp / row_total
    zero_grads = jnp.zeros((BATCH, D_EMB), jnp.float32)

    def group_pass(grad_passage, group_index):

        def backward_pass(carried, sub_index):
            plain_acc, mixed_acc = carried
            block_index = group_index * per_group + sub_index
            first_row, row_ids, query_part, score_tile, diagonal = score_block(block_index)
            exp_tile = jnp.exp(score_tile - inverse_temp)
            target_twice = jnp.where(diagonal, 2.0, 0.0)
            row_part = lax.dynamic_slice_in_dim(row_total, first_row, block_rows, 0)
            exp_low = exp_tile.astype(jnp.bfloat16)
            column_low = (exp_tile / column_total[None, :] - target_twice).astype(jnp.bfloat16)
            row_low = (exp_tile / row_part[:, None] - target_twice).astype(jnp.bfloat16)
            plain_parts = jnp.einsum('rcp,cpd->rcd', exp_low.astype(jnp.float32).reshape(block_rows, N_PA, PBLOCK), p_blocks)
            mixed_parts = jnp.einsum('rcp,cpd->rcd', column_low.astype(jnp.float32).reshape(block_rows, N_PA, PBLOCK), p_blocks)
            hard_share = lax.dynamic_slice_in_dim(hard_weight, first_row, block_rows, 0)
            hard_part = lax.dynamic_slice_in_dim(hard_picked, first_row, block_rows, 0).astype(jnp.float32)
            owner = ((row_ids // PBLOCK)[:, None] == block_names[None, :]).astype(jnp.float32)
            hard_term = owner[:, :, None] * (hard_share[:, None] * hard_part)[:, None, :]
            parts = inverse_temp * (plain_parts / row_part[:, None, None] + mixed_parts + hard_term)
            grad_question = lax.optimization_barrier(jnp.sum(round_low(parts), axis=1))
            plain_acc = plain_acc + jnp.dot(exp_low.T, query_part, preferred_element_type=jnp.float32)
            mixed_acc = mixed_acc + jnp.dot(row_low.T, query_part, preferred_element_type=jnp.float32)
            return ((plain_acc, mixed_acc), grad_question)
        sub_ids = jnp.arange(per_group, dtype=jnp.int32)
        (plain_acc, mixed_acc), grad_question = lax.scan(backward_pass, (zero_grads, zero_grads), sub_ids)
        passage_part = round_low(inverse_temp * (plain_acc / column_total[:, None] + mixed_acc))
        return (grad_passage + passage_part, grad_question)
    group_ids = jnp.arange(N_PB, dtype=jnp.int32)
    grad_passage, grad_question = lax.scan(group_pass, zero_grads, group_ids)
    grad_question = grad_question.reshape(BATCH, D_EMB)
    grad_hard_unit = round_low(inverse_temp * zero_grads.at[hard_index].add(hard_weight[:, None] * q_low.astype(jnp.float32)))
    q_back = unit_grad(grad_question, q_unit, q_norm)
    p_back = unit_grad(grad_passage, p_unit, p_norm)
    h_back = unit_grad(grad_hard_unit, h_unit, h_norm)
    flipped = projection.T
    grad_questions = jnp.dot(q_back, flipped, preferred_element_type=jnp.float32).astype(jnp.bfloat16)
    grad_passages = jnp.dot(p_back, flipped, preferred_element_type=jnp.float32).astype(jnp.bfloat16)
    grad_hard = jnp.dot(h_back, flipped, preferred_element_type=jnp.float32).astype(jnp.bfloat16)
    return (grad_questions, grad_passages, grad_hard, question_loss, passage_loss)
```

```python
import jax
import jax.numpy as jnp
from jax import lax
from jax.experimental import pallas as pl
from jax.experimental.pallas import tpu as pltpu
from jax.sharding import PartitionSpec as P

inverse_temp = 40.0
epsilon = 1e-06
f32 = jnp.float32
bf16 = jnp.bfloat16

NZ, NX, NY = 8, 4, 4
ROWS = 64
HALF = 32
GROUP = 1024
WIDTH = 768
MODEL = 4096
CHUNK = 512
TILE = 256


def nt(a, b):
    return lax.dot_general(a, b, (((1,), (1,)), ((), ())), preferred_element_type=f32)


def tn(a, b):
    return lax.dot_general(a, b, (((0,), (0,)), ((), ())), preferred_element_type=f32)


def wide(column, times):
    return jnp.concatenate([column] * times, axis=1)


def kernel(
    xq_ref, xp_ref, xh_ref, idx_ref, w_ref,
    oq_ref, op_ref, oh_ref, lq_ref, lp_ref,
    xs, w, acc, unit, scale, q_all, p_all, h_own, h_all, h_pick, gh_out, gh_in,
    e_s, g_s, tile_s, csum, tq, tp, rcol, crow, hcol, loss_s,
    dq, prt, zl_in, zs_in, dpa, dpb, a1, b1, a2, b2, ge,
    in_sem, w_sem, send, recv, tq_send, tq_recv, tp_send, tp_recv, h_sem, hg_sem, pt_send, pt_recv,
):
    pb, pa = lax.axis_index("pb"), lax.axis_index("pa")
    x, y_lo = pb // 2, pb % 2
    y_hi, z, core = pa // 16, (pa // 2) % 8, pa % 2
    y = y_hi * 2 + y_lo
    d = 1 - 2 * core

    def device(xx, yy, zz, cc):
        return (xx * 2 + yy % 2, (yy // 2) * 16 + zz * 2 + cc)

    def zmod(v):
        return (v + 16) % 8

    def mod4(v):
        return (v + 8) % 4

    q_slot = z * 2 + core
    p_slot = y_hi * 8 + pb

    def q_peer(s):
        return (pb, y_hi * 16 + s)

    def p_peer(s):
        return (s % 8, (s // 8) * 16 + q_slot)

    def slot_of(xx, yy):
        return (yy // 2) * 8 + xx * 2 + yy % 2

    def rows(ref, slot, first=0, count=ROWS):
        return ref.at[pl.ds(pl.multiple_of(slot * ROWS + first, HALF), count)]

    counter = [0]
    started = []

    def remote(src, dst, to):
        n = counter[0]
        counter[0] += 1
        copy = pltpu.make_async_remote_copy(
            src_ref=src, dst_ref=dst, send_sem=send.at[n], recv_sem=recv.at[n],
            device_id=to, device_id_type=pl.DeviceIdType.MESH,
        )
        copy.start()
        started.append(copy)
        return n

    def arrive(n, dst):
        pltpu.make_async_remote_copy(
            src_ref=dst, dst_ref=dst, send_sem=send.at[n], recv_sem=recv.at[n],
            device_id=(pb, pa), device_id_type=pl.DeviceIdType.MESH,
        ).wait_recv()

    inputs = []
    for i, ref in enumerate((xq_ref, xp_ref, xh_ref)):
        copy = pltpu.make_async_copy(ref, xs.at[pl.ds(i * ROWS, ROWS)], in_sem.at[i])
        copy.start()
        inputs.append(copy)
    for k in range(MODEL // CHUNK):
        pltpu.make_async_copy(w_ref.at[pl.ds(k * CHUNK, CHUNK)], w.at[pl.ds(k * CHUNK, CHUNK)], w_sem.at[k]).start()

    barrier = pltpu.get_barrier_semaphore()

    def greet(k, carry):
        pl.semaphore_signal(barrier, inc=1, device_id=q_peer((q_slot + k) % 16), device_id_type=pl.DeviceIdType.MESH)
        pl.semaphore_signal(barrier, inc=1, device_id=p_peer((p_slot + k) % 16), device_id_type=pl.DeviceIdType.MESH)
        return carry

    lax.fori_loop(1, 16, greet, 0)

    for copy in inputs:
        copy.wait()
    acc[...] = jnp.zeros_like(acc)

    def project(k, carry):
        first = pl.multiple_of(k * CHUNK, CHUNK)
        pltpu.make_async_copy(w_ref.at[pl.ds(first, CHUNK)], w.at[pl.ds(first, CHUNK)], w_sem.at[k]).wait()
        acc[...] += jnp.dot(xs[:, pl.ds(first, CHUNK)], w[pl.ds(first, CHUNK), :], preferred_element_type=f32)
        return carry

    lax.fori_loop(0, MODEL // CHUNK, project, 0)

    def normalise(i):
        emb = acc[i * ROWS : (i + 1) * ROWS, :]
        s = lax.rsqrt(jnp.sum(emb * emb, axis=1, keepdims=True) + epsilon)
        u = emb * s
        scale[i * ROWS : (i + 1) * ROWS, :] = jnp.broadcast_to(s, (ROWS, 128))
        unit[i * ROWS : (i + 1) * ROWS, :] = u
        return u.astype(bf16)

    q_all[pl.ds(pl.multiple_of(q_slot * ROWS, ROWS), ROWS), :] = normalise(0)
    p_all[pl.ds(pl.multiple_of(p_slot * ROWS, ROWS), ROWS), :] = normalise(1)
    h_own[...] = normalise(2)
    pl.semaphore_wait(barrier, 30)

    long_to = device(x, y, zmod(z + d), core)
    short_to = device(x, y, zmod(z - d), core)
    other = device(x, y, z, 1 - core)
    xl, xr, yl, yr = mod4(x + d), mod4(x - d), mod4(y + d), mod4(y - d)
    x2, y2 = mod4(x + 2), mod4(y + 2)
    to_xl, to_xr = device(xl, y, z, core), device(xr, y, z, core)
    to_yl, to_yr = device(x, yl, z, core), device(x, yr, z, core)

    def qz(zz, cc):
        return zmod(zz) * 2 + cc

    def push(ref, slot, to, first=0, count=ROWS):
        part = rows(ref, slot, first, count)
        return remote(part, part, to)

    def await_rows(n, ref, slot, first=0, count=ROWS):
        arrive(n, rows(ref, slot, first, count))

    q_long, q_short, q_other, other_slots = [], [], [], []
    for hf in range(2):
        q_long.append(push(q_all, q_slot, long_to, hf * HALF, HALF))
        q_short.append(push(q_all, q_slot, short_to, hf * HALF, HALF))
    p_from_xr = push(p_all, p_slot, to_xl)
    p_from_xl = push(p_all, p_slot, to_xr)
    p_from_yr = push(p_all, p_slot, to_yl)
    p_from_yl = push(p_all, p_slot, to_yr)
    q_other.append(push(q_all, q_slot, other))
    other_slots.append(qz(z, 1 - core))

    keeper = y_hi * 8 + z
    keeper_dev = (keeper // 2, (keeper % 2) * 16 + q_slot)
    is_keeper = z == (2 * pb + y_hi) % 8
    kb = (2 * pb + y_hi) // 8
    ka = core
    sends_hard = jnp.logical_not(jnp.logical_and(is_keeper, kb == y_hi))

    @pl.when(sends_hard)
    def _():
        part = rows(h_all, pb)
        pltpu.make_async_remote_copy(
            src_ref=h_own, dst_ref=part, send_sem=h_sem.at[8], recv_sem=h_sem.at[pb],
            device_id=keeper_dev, device_id_type=pl.DeviceIdType.MESH,
        ).start()

    @pl.when(jnp.logical_not(sends_hard))
    def _():
        h_all[pl.ds(pl.multiple_of(pb * ROWS, ROWS), ROWS), :] = h_own[...]

    def q_wave(step):
        nonlocal q_long, q_short
        nl, ns = [], []
        for hf in range(2):
            slot = qz(z - (step + 1) * d, core)
            await_rows(q_long[hf], q_all, slot, hf * HALF, HALF)
            if step < 3:
                nl.append(push(q_all, slot, long_to, hf * HALF, HALF))
            if step < 3:
                slot2 = qz(z + (step + 1) * d, core)
                await_rows(q_short[hf], q_all, slot2, hf * HALF, HALF)
                if step < 2:
                    ns.append(push(q_all, slot2, short_to, hf * HALF, HALF))
        q_other.append(push(q_all, slot, other))
        other_slots.append(qz(z + (step + 1) * d, 1 - core))
        if step < 3:
            q_other.append(push(q_all, slot2, other))
            other_slots.append(qz(z - (step + 1) * d, 1 - core))
        q_long, q_short = nl, ns

    A, B = 0, HALF
    q_wave(0)
    await_rows(p_from_xr, p_all, slot_of(xr, y))
    n_x2 = push(p_all, slot_of(xr, y), to_xl)
    await_rows(p_from_yr, p_all, slot_of(x, yr))
    n_y2 = push(p_all, slot_of(x, yr), to_yl)
    n_xr_yl = push(p_all, slot_of(xr, y), to_yl, A, HALF)
    n_xr_yr = push(p_all, slot_of(xr, y), to_yr, A, HALF)
    m_yr_xl = push(p_all, slot_of(x, yr), to_xl, B, HALF)
    m_yr_xr = push(p_all, slot_of(x, yr), to_xr, B, HALF)
    await_rows(p_from_xl, p_all, slot_of(xl, y))
    n_xl_yl = push(p_all, slot_of(xl, y), to_yl, A, HALF)
    n_xl_yr = push(p_all, slot_of(xl, y), to_yr, A, HALF)
    await_rows(p_from_yl, p_all, slot_of(x, yl))
    m_yl_xl = push(p_all, slot_of(x, yl), to_xl, B, HALF)
    m_yl_xr = push(p_all, slot_of(x, yl), to_xr, B, HALF)
    q_wave(1)
    await_rows(n_xr_yl, p_all, slot_of(xr, yr), A, HALF)
    k_xr = push(p_all, slot_of(xr, yr), to_yl, A, HALF)
    await_rows(m_yr_xl, p_all, slot_of(xr, yr), B, HALF)
    l_yr = push(p_all, slot_of(xr, yr), to_xl, B, HALF)
    await_rows(n_xl_yl, p_all, slot_of(xl, yr), A, HALF)
    k_xl = push(p_all, slot_of(xl, yr), to_yl, A, HALF)
    await_rows(m_yl_xl, p_all, slot_of(xr, yl), B, HALF)
    l_yl = push(p_all, slot_of(xr, yl), to_xl, B, HALF)
    await_rows(n_x2, p_all, slot_of(x2, y))
    n_x2_yl = push(p_all, slot_of(x2, y), to_yl, A, HALF)
    n_x2_yr = push(p_all, slot_of(x2, y), to_yr, A, HALF)
    await_rows(n_y2, p_all, slot_of(x, y2))
    m_y2_xl = push(p_all, slot_of(x, y2), to_xl, B, HALF)
    m_y2_xr = push(p_all, slot_of(x, y2), to_xr, B, HALF)
    q_wave(2)
    await_rows(n_x2_yl, p_all, slot_of(x2, yr), A, HALF)
    k_x2 = push(p_all, slot_of(x2, yr), to_yl, A, HALF)
    await_rows(m_y2_xl, p_all, slot_of(xr, y2), B, HALF)
    l_y2 = push(p_all, slot_of(xr, y2), to_xl, B, HALF)
    await_rows(n_xr_yr, p_all, slot_of(xr, yl), A, HALF)
    await_rows(n_xl_yr, p_all, slot_of(xl, yl), A, HALF)
    await_rows(m_yr_xr, p_all, slot_of(xl, yr), B, HALF)
    await_rows(m_yl_xr, p_all, slot_of(xl, yl), B, HALF)
    q_wave(3)
    await_rows(n_x2_yr, p_all, slot_of(x2, yl), A, HALF)
    await_rows(m_y2_xr, p_all, slot_of(xl, y2), B, HALF)
    await_rows(k_xr, p_all, slot_of(xr, y2), A, HALF)
    await_rows(k_xl, p_all, slot_of(xl, y2), A, HALF)
    await_rows(l_yr, p_all, slot_of(x2, yr), B, HALF)
    await_rows(l_yl, p_all, slot_of(x2, yl), B, HALF)
    await_rows(k_x2, p_all, slot_of(x2, y2), A, HALF)
    await_rows(l_y2, p_all, slot_of(x2, y2), B, HALF)
    for n, slot in zip(q_other, other_slots):
        await_rows(n, q_all, slot)

    csum[...] = jnp.zeros_like(csum)
    tq[q_slot] = jnp.zeros((16, 128), f32)
    tp[p_slot] = jnp.zeros((16, 128), f32)

    def score(t, carry):
        first = pl.multiple_of(t * TILE, TILE)
        s = nt(q_all[pl.ds(first, TILE), :], p_all[...])
        e = jnp.exp(inverse_temp * s - inverse_temp)
        e_s[pl.ds(first, TILE), :] = e
        csum[...] += jnp.sum(e.reshape(TILE // 8, 8, GROUP), axis=0)
        part = e[:, :128]
        for j in range(1, GROUP // 128):
            part = part + e[:, j * 128 : (j + 1) * 128]
        for j in range(TILE // 128):
            row = jnp.sum(jnp.transpose(part[j * 128 : (j + 1) * 128, :]), axis=0, keepdims=True)
            tq[q_slot, pl.ds(t * (TILE // 128) + j, 1), :] = row
        return carry

    lax.fori_loop(0, GROUP // TILE, score, 0)
    total = jnp.sum(csum[...], axis=0, keepdims=True)
    for j in range(GROUP // 128):
        tp[p_slot, pl.ds(j, 1), :] = total[:, j * 128 : (j + 1) * 128]

    eye = lax.broadcasted_iota(jnp.int32, (128, 128), 0) == lax.broadcasted_iota(jnp.int32, (128, 128), 1)

    def paired(a, b):
        return jnp.sum(jnp.where(eye, inverse_temp * nt(a, b), 0.0), axis=0, keepdims=True)

    @pl.when(is_keeper)
    def _():
        for s in range(8):
            @pl.when(jnp.logical_not(jnp.logical_and(kb == y_hi, pb == s)))
            def _():
                part = h_all.at[pl.ds(s * ROWS, ROWS)]
                pltpu.make_async_remote_copy(
                    src_ref=part, dst_ref=part, send_sem=h_sem.at[8], recv_sem=h_sem.at[s],
                    device_id=(pb, pa), device_id_type=pl.DeviceIdType.MESH,
                ).wait_recv()
        block_base = (kb * 16 + q_slot) * 512
        hidx = idx_ref[y_hi * 2 + ka] - block_base
        for j in range(4):
            hit = lax.broadcasted_iota(jnp.int32, (512, 128), 0) == hidx[j : j + 1, :]
            pick = tn(hit.astype(bf16), h_all[...]).astype(bf16)
            h_pick[j * 128 : (j + 1) * 128, :] = pick
            q_rows = q_all[pl.ds(pl.multiple_of(ka * 512 + j * 128, 128), 128), :]
            p_rows = p_all[pl.ds(pl.multiple_of(kb * 512 + j * 128, 128), 128), :]
            he = jnp.exp(paired(q_rows, pick) - inverse_temp)
            hcol[pl.ds(j, 1), :] = he
            tq[q_slot, pl.ds(ka * 4 + j, 1), :] += he
            diag = paired(q_rows, p_rows)
            tq[q_slot, pl.ds(8 + ka * 4 + j, 1), :] = diag
            tp[p_slot, pl.ds(8 + kb * 4 + j, 1), :] = diag

    def tell(k, carry):
        pltpu.make_async_remote_copy(
            src_ref=tq.at[q_slot], dst_ref=tq.at[q_slot], send_sem=tq_send.at[k], recv_sem=tq_recv.at[q_slot],
            device_id=q_peer((q_slot + k) % 16), device_id_type=pl.DeviceIdType.MESH,
        ).start()
        pltpu.make_async_remote_copy(
            src_ref=tp.at[p_slot], dst_ref=tp.at[p_slot], send_sem=tp_send.at[k], recv_sem=tp_recv.at[p_slot],
            device_id=p_peer((p_slot + k) % 16), device_id_type=pl.DeviceIdType.MESH,
        ).start()
        return carry

    def heard(k, carry):
        sq, sp = (q_slot + k) % 16, (p_slot + k) % 16
        pltpu.make_async_remote_copy(
            src_ref=tq.at[q_slot], dst_ref=tq.at[sq], send_sem=tq_send.at[k], recv_sem=tq_recv.at[sq],
            device_id=(pb, pa), device_id_type=pl.DeviceIdType.MESH,
        ).wait()
        pltpu.make_async_remote_copy(
            src_ref=tp.at[p_slot], dst_ref=tp.at[sp], send_sem=tp_send.at[k], recv_sem=tp_recv.at[sp],
            device_id=(pb, pa), device_id_type=pl.DeviceIdType.MESH,
        ).wait()
        return carry

    lax.fori_loop(1, 16, tell, 0)
    lax.fori_loop(1, 16, heard, 0)
    sq = jnp.sum(tq[...], axis=0)
    sp = jnp.sum(tp[...], axis=0)
    loss_s[0:8, :] = inverse_temp + jnp.log(sq[:8]) - sq[8:]
    loss_s[8:16, :] = inverse_temp + jnp.log(sp[:8]) - sp[8:]
    rinv = inverse_temp / sq[:8]
    cinv = inverse_temp / sp[:8]
    for j in range(8):
        rcol[j * 128 : (j + 1) * 128, :] = jnp.transpose(jnp.broadcast_to(rinv[j : j + 1, :], (128, 128)))
        crow[:, j * 128 : (j + 1) * 128] = jnp.broadcast_to(cinv[j : j + 1, :], (8, 128))
    lrow = loss_s[pl.ds(z, 1), :]
    lq_ref[...] = jnp.where(core == 0, lrow[:, :ROWS], lrow[:, ROWS:])
    lrow = loss_s[pl.ds(8 + y_hi * 4 + x, 1), :]
    lp_ref[...] = jnp.where(y_lo == 0, lrow[:, :ROWS], lrow[:, ROWS:])

    def weigh(t, carry):
        first = pl.multiple_of(t * TILE, TILE)
        factor = wide(rcol[pl.ds(first, TILE), :], GROUP // 128) + crow[0:1, :]
        g_s[pl.ds(first, TILE), :] = (e_s[pl.ds(first, TILE), :] * factor).astype(bf16)
        return carry

    lax.fori_loop(0, GROUP // TILE, weigh, 0)

    @pl.when(is_keeper)
    def _():
        for j in range(4):
            r = pl.multiple_of(ka * 512 + j * 128, 128)
            c = pl.multiple_of(kb * 512 + j * 128, 128)
            factor = rcol[pl.ds(r, 128), :] + crow[0:1, pl.ds(c, 128)]
            value = e_s[pl.ds(r, 128), pl.ds(c, 128)] * factor - jnp.where(eye, 2.0 * inverse_temp, 0.0)
            g_s[pl.ds(r, 128), pl.ds(c, 128)] = value.astype(bf16)
            share = jnp.transpose(jnp.broadcast_to(hcol[j : j + 1, :], (128, 128))) * rcol[pl.ds(r, 128), :]
            gh_in[j * 128 : (j + 1) * 128, :] = wide(share, WIDTH // 128) * q_all[pl.ds(r, 128), :].astype(f32)
            h_pick_f = wide(share, WIDTH // 128) * h_pick[j * 128 : (j + 1) * 128, :].astype(f32)
            tile_s[j * 128 : (j + 1) * 128, :] = h_pick_f
        hidx = idx_ref[y_hi * 2 + ka] - (kb * 16 + q_slot) * 512
        total_h = jnp.zeros((512, WIDTH), f32)
        for j in range(4):
            hit = lax.broadcasted_iota(jnp.int32, (512, 128), 0) == hidx[j : j + 1, :]
            total_h = total_h + jnp.dot(
                hit.astype(bf16), gh_in[j * 128 : (j + 1) * 128, :].astype(bf16), preferred_element_type=f32
            )
        gh_out[0:512, :] = total_h.astype(bf16)
        for s in range(8):
            here = jnp.logical_and(kb == y_hi, pb == s)

            @pl.when(jnp.logical_not(here))
            def _():
                pltpu.make_async_remote_copy(
                    src_ref=gh_out.at[pl.ds(s * ROWS, ROWS)], dst_ref=gh_out.at[pl.ds(512, ROWS)],
                    send_sem=hg_sem.at[s], recv_sem=hg_sem.at[8],
                    device_id=(s, kb * 16 + q_slot), device_id_type=pl.DeviceIdType.MESH,
                ).start()

            @pl.when(here)
            def _():
                gh_out[512 : 512 + ROWS, :] = gh_out[s * ROWS : (s + 1) * ROWS, :]

    t0 = zmod(z + 4) // 2

    def question_tile(i, carry):
        t = (t0 + i) % 4
        first = pl.multiple_of(t * TILE, TILE)
        value = jnp.dot(g_s[pl.ds(first, TILE), :], p_all[...], preferred_element_type=f32)

        @pl.when(jnp.logical_and(is_keeper, t // 2 == ka))
        def _():
            at = pl.multiple_of((t % 2) * TILE, TILE)
            summed = value + tile_s[pl.ds(at, TILE), :]
            for j in range(4):
                dq[j % 2, t * 2 + j // 2] = summed[j * ROWS : (j + 1) * ROWS, :].astype(bf16)

        @pl.when(jnp.logical_not(jnp.logical_and(is_keeper, t // 2 == ka)))
        def _():
            for j in range(4):
                dq[j % 2, t * 2 + j // 2] = value[j * ROWS : (j + 1) * ROWS, :].astype(bf16)

        pltpu.make_async_remote_copy(
            src_ref=dq.at[1 - core, pl.ds(t * 2, 2)], dst_ref=prt.at[pl.ds(t * 2, 2)],
            send_sem=pt_send.at[t], recv_sem=pt_recv.at[t],
            device_id=other, device_id_type=pl.DeviceIdType.MESH,
        ).start()
        return carry

    lax.fori_loop(0, 4, question_tile, 0)

    def passage_tile(t, carry):
        first = pl.multiple_of(t * TILE, TILE)
        value = tn(g_s[:, pl.ds(first, TILE)], q_all[...]).astype(bf16)
        for j in range(4):
            slot = t * 4 + j
            yy = (slot // 8) * 2 + j % 2
            xx = (slot % 8) // 2
            dpa[yy, xx] = value[j * ROWS : j * ROWS + HALF, :]
            dpb[xx, yy] = value[j * ROWS + HALF : (j + 1) * ROWS, :]
        return carry

    lax.fori_loop(0, 4, passage_tile, 0)

    n_a1 = remote(dpa.at[y2], a1.at[0], to_yl)
    n_b1 = remote(dpb.at[x2], b1.at[0], to_xl)
    n_a1s = remote(dpa.at[yr], a1.at[1], to_yr)
    n_b1s = remote(dpb.at[xr], b1.at[1], to_xr)

    def own_sum(k, carry):
        t = k
        pltpu.make_async_remote_copy(
            src_ref=dq.at[1 - core, pl.ds(t * 2, 2)], dst_ref=prt.at[pl.ds(t * 2, 2)],
            send_sem=pt_send.at[t], recv_sem=pt_recv.at[t],
            device_id=other, device_id_type=pl.DeviceIdType.MESH,
        ).wait()
        prt[pl.ds(t * 2, 2)] = (
            prt[pl.ds(t * 2, 2)].astype(f32) + dq[core, pl.ds(t * 2, 2)].astype(f32)
        ).astype(bf16)
        return carry

    lax.fori_loop(0, 4, own_sum, 0)

    def half(ref, hf):
        return ref.at[pl.ds(hf * HALF, HALF)]

    r_long, r_short = [], []
    for hf in range(2):
        r_long.append(remote(half(prt.at[zmod(z + 4)], hf), half(zl_in.at[0], hf), long_to))
        r_short.append(remote(half(prt.at[zmod(z - 3 * d)], hf), half(zs_in.at[0], hf), short_to))

    def q_back(step):
        nonlocal r_long, r_short
        nl, ns = [], []
        for hf in range(2):
            part = slice(hf * HALF, (hf + 1) * HALF)
            arrive(r_long[hf], half(zl_in.at[step], hf))
            if step < 3:
                mine = prt[zmod(z + (3 - step) * d), part, :].astype(f32)
                zl_in[step, part, :] = (zl_in[step, part, :].astype(f32) + mine).astype(bf16)
                nl.append(remote(half(zl_in.at[step], hf), half(zl_in.at[step + 1], hf), long_to))
            if step < 3:
                arrive(r_short[hf], half(zs_in.at[step], hf))
            if step < 2:
                mine = prt[zmod(z - (2 - step) * d), part, :].astype(f32)
                zs_in[step, part, :] = (zs_in[step, part, :].astype(f32) + mine).astype(bf16)
                ns.append(remote(half(zs_in.at[step], hf), half(zs_in.at[step + 1], hf), short_to))
        r_long, r_short = nl, ns

    q_back(0)
    arrive(n_a1, a1.at[0])
    a1[0] = (a1[0].astype(f32) + dpa[yl].astype(f32)).astype(bf16)
    n_a1l = remote(a1.at[0], a1.at[2], to_yl)
    arrive(n_b1, b1.at[0])
    b1[0] = (b1[0].astype(f32) + dpb[xl].astype(f32)).astype(bf16)
    n_b1l = remote(b1.at[0], b1.at[2], to_xl)
    q_back(1)
    arrive(n_a1s, a1.at[1])
    arrive(n_a1l, a1.at[2])
    a1[1] = (a1[1].astype(f32) + a1[2].astype(f32) + dpa[y].astype(f32)).astype(bf16)
    n_a2 = remote(a1.at[1, x2], a2.at[0], to_xl)
    n_a2s = remote(a1.at[1, xr], a2.at[1], to_xr)
    arrive(n_b1s, b1.at[1])
    arrive(n_b1l, b1.at[2])
    b1[1] = (b1[1].astype(f32) + b1[2].astype(f32) + dpb[x].astype(f32)).astype(bf16)
    n_b2 = remote(b1.at[1, y2], b2.at[0], to_yl)
    n_b2s = remote(b1.at[1, yr], b2.at[1], to_yr)
    q_back(2)
    arrive(n_a2, a2.at[0])
    a2[0] = (a2[0].astype(f32) + a1[1, xl].astype(f32)).astype(bf16)
    n_a2l = remote(a2.at[0], a2.at[2], to_xl)
    arrive(n_b2, b2.at[0])
    b2[0] = (b2[0].astype(f32) + b1[1, yl].astype(f32)).astype(bf16)
    n_b2l = remote(b2.at[0], b2.at[2], to_yl)

    def back(grad, i, first, count):
        part = slice(i * ROWS + first, i * ROWS + first + count)
        u = unit[part, :]
        along = jnp.sum(grad * u, axis=1, keepdims=True)
        ge[part, :] = ((grad - u * along) * wide(scale[part, :], WIDTH // 128)).astype(bf16)

    @pl.when(sends_hard)
    def _():
        pltpu.make_async_remote_copy(
            src_ref=gh_out.at[pl.ds(0, ROWS)], dst_ref=gh_out.at[pl.ds(512, ROWS)],
            send_sem=hg_sem.at[0], recv_sem=hg_sem.at[8],
            device_id=(pb, pa), device_id_type=pl.DeviceIdType.MESH,
        ).wait_recv()

    back(gh_out[512 : 512 + ROWS, :].astype(f32), 2, 0, ROWS)

    q_back(3)
    grad_q = prt[z].astype(f32) + zl_in[3].astype(f32) + zs_in[2].astype(f32)
    back(grad_q, 0, 0, ROWS)
    arrive(n_a2s, a2.at[1])
    arrive(n_a2l, a2.at[2])
    back(a2[1].astype(f32) + a2[2].astype(f32) + a1[1, x].astype(f32), 1, 0, HALF)
    arrive(n_b2s, b2.at[1])
    arrive(n_b2l, b2.at[2])
    back(b2[1].astype(f32) + b2[2].astype(f32) + b1[1, y].astype(f32), 1, HALF, HALF)

    def unproject(k, carry):
        first = pl.multiple_of(k * CHUNK, CHUNK)
        value = nt(ge[...], w[pl.ds(first, CHUNK), :]).astype(bf16)
        oq_ref[:, pl.ds(first, CHUNK)] = value[:ROWS]
        op_ref[:, pl.ds(first, CHUNK)] = value[ROWS : 2 * ROWS]
        oh_ref[:, pl.ds(first, CHUNK)] = value[2 * ROWS :]
        return carry

    lax.fori_loop(0, MODEL // CHUNK, unproject, 0)

    for copy in started:
        copy.wait_send()

    @pl.when(sends_hard)
    def _():
        pltpu.make_async_remote_copy(
            src_ref=h_own, dst_ref=rows(h_all, pb), send_sem=h_sem.at[8], recv_sem=h_sem.at[pb],
            device_id=keeper_dev, device_id_type=pl.DeviceIdType.MESH,
        ).wait_send()

    @pl.when(is_keeper)
    def _():
        for s in range(8):
            @pl.when(jnp.logical_not(jnp.logical_and(kb == y_hi, pb == s)))
            def _():
                pltpu.make_async_remote_copy(
                    src_ref=gh_out.at[pl.ds(s * ROWS, ROWS)], dst_ref=gh_out.at[pl.ds(512, ROWS)],
                    send_sem=hg_sem.at[s], recv_sem=hg_sem.at[8],
                    device_id=(s, kb * 16 + q_slot), device_id_type=pl.DeviceIdType.MESH,
                ).wait_send()


COPIES = 110


def shards(questions, passages, hard_rows, hard_index, projection):
    vmem = pl.BlockSpec(memory_space=pltpu.VMEM)
    hbm = pl.BlockSpec(memory_space=pl.ANY)
    out = jax.ShapeDtypeStruct((ROWS, MODEL), bf16)
    loss = jax.ShapeDtypeStruct((1, ROWS), f32)
    V, D = pltpu.VMEM, pltpu.SemaphoreType.DMA
    gq, gp, gh, lq, lp = pl.pallas_call(
        kernel,
        out_shape=(out, out, out, loss, loss),
        in_specs=[hbm, hbm, hbm, vmem, hbm],
        out_specs=(vmem,) * 5,
        scratch_shapes=[
            V((3 * ROWS, MODEL), bf16),
            V((MODEL, WIDTH), bf16),
            V((3 * ROWS, WIDTH), f32),
            V((3 * ROWS, WIDTH), f32),
            V((3 * ROWS, 128), f32),
            V((GROUP, WIDTH), bf16),
            V((GROUP, WIDTH), bf16),
            V((ROWS, WIDTH), bf16),
            V((512, WIDTH), bf16),
            V((512, WIDTH), bf16),
            V((512 + ROWS, WIDTH), bf16),
            V((512, WIDTH), f32),
            V((GROUP, GROUP), f32),
            V((GROUP, GROUP), bf16),
            V((512, WIDTH), f32),
            V((8, GROUP), f32),
            V((16, 16, 128), f32),
            V((16, 16, 128), f32),
            V((GROUP, 128), f32),
            V((8, GROUP), f32),
            V((8, 128), f32),
            V((16, 128), f32),
            V((2, 8, ROWS, WIDTH), bf16),
            V((8, ROWS, WIDTH), bf16),
            V((4, ROWS, WIDTH), bf16),
            V((3, ROWS, WIDTH), bf16),
            V((4, 4, HALF, WIDTH), bf16),
            V((4, 4, HALF, WIDTH), bf16),
            V((3, 4, HALF, WIDTH), bf16),
            V((3, 4, HALF, WIDTH), bf16),
            V((3, HALF, WIDTH), bf16),
            V((3, HALF, WIDTH), bf16),
            V((3 * ROWS, WIDTH), bf16),
            D((3,)), D((MODEL // CHUNK,)),
            D((COPIES,)), D((COPIES,)),
            D((16,)), D((16,)), D((16,)), D((16,)),
            D((9,)), D((9,)), D((4,)), D((4,)),
        ],
        compiler_params=pltpu.CompilerParams(
            collective_id=0, has_side_effects=True, vmem_limit_bytes=56 * 1024 * 1024
        ),
        cost_estimate=pl.CostEstimate(flops=8 * 10**9, bytes_accessed=10**7, transcendentals=10**6),
    )(questions, passages, hard_rows, hard_index.reshape(4, 4, 128), projection)
    return gq, gp, gh, lq.reshape(ROWS), lp.reshape(ROWS)


def solution(mesh):
    in_specs = (P(("pb", "pa"), None), P(("pa", "pb"), None), P(("pa", "pb"), None), P("pb"), P())
    out_specs = (
        P(("pb", "pa"), None),
        P(("pa", "pb"), None),
        P(("pa", "pb"), None),
        P(("pb", "pa")),
        P(("pa", "pb")),
    )
    return jax.shard_map(shards, mesh=mesh, in_specs=in_specs, out_specs=out_specs, check_vma=False)
```

```python
import jax
import jax.numpy as jnp
from jax import lax
from jax.experimental import pallas as pl
from jax.experimental.pallas import tpu as pltpu
from jax.sharding import PartitionSpec as P

inverse_temp = 40.0
epsilon = 1e-06
f32 = jnp.float32
bf16 = jnp.bfloat16

NZ, NX, NY = 8, 4, 4
ROWS = 64
HALF = 32
GROUP = 1024
WIDTH = 768
MODEL = 4096
CHUNK = 1024
TILE = 256


def nt(a, b):
    return lax.dot_general(a, b, (((1,), (1,)), ((), ())), preferred_element_type=f32)


def tn(a, b):
    return lax.dot_general(a, b, (((0,), (0,)), ((), ())), preferred_element_type=f32)


def wide(column, times):
    return jnp.concatenate([column] * times, axis=1)


def kernel(
    xq_ref, xp_ref, xh_ref, idx_ref, w_ref,
    oq_ref, op_ref, oh_ref, lq_ref, lp_ref,
    xs, w, wt, acc, unit, scale, q_all, p_all, h_own, h_rel, h_in, dh_out, dh_rel, dh_in, eh, gh,
    e_s, g_s, tile_s, csum, tq, tp, rcol, crow, rin_s, dg, dgq, dgp, lrow_s,
    dq, prt, zr, zin, dpa, dpb, a1, b1, a2, b2, ge, out_s,
    idx_s, loss_s,
    in_sem, w_sem, send, recv, tq_send, tq_recv, tp_send, tp_recv, dg_send, dg_recv, hop_sem, pt_send, pt_recv, o_sem,
):
    pb, pa = lax.axis_index("pb"), lax.axis_index("pa")
    x, y_lo = pb // 2, pb % 2
    y_hi, z, core = pa // 16, (pa // 2) % 8, pa % 2
    y = y_hi * 2 + y_lo
    d = 1 - 2 * core

    def device(xx, yy, zz, cc):
        return (xx * 2 + yy % 2, (yy // 2) * 16 + zz * 2 + cc)

    def zmod(v):
        return (v + 16) % 8

    def mod4(v):
        return (v + 8) % 4

    q_slot = z * 2 + core
    p_slot = y_hi * 8 + pb

    def q_slot_of(zz):
        return zz * 2 + core

    def q_peer(s):
        return (pb, y_hi * 16 + s)

    def p_peer(s):
        return (s % 8, (s // 8) * 16 + q_slot)

    def slot_of(xx, yy):
        return (yy // 2) * 8 + xx * 2 + yy % 2

    def rows(ref, slot, first=0, count=ROWS):
        return ref.at[pl.ds(pl.multiple_of(slot * ROWS + first, HALF), count)]

    counter = [0]
    started = []

    def remote(src, dst, to):
        n = counter[0]
        counter[0] += 1
        copy = pltpu.make_async_remote_copy(
            src_ref=src, dst_ref=dst, send_sem=send.at[n], recv_sem=recv.at[n],
            device_id=to, device_id_type=pl.DeviceIdType.MESH,
        )
        copy.start()
        started.append(copy)
        return n

    def arrive(n, dst):
        pltpu.make_async_remote_copy(
            src_ref=dst, dst_ref=dst, send_sem=send.at[n], recv_sem=recv.at[n],
            device_id=(pb, pa), device_id_type=pl.DeviceIdType.MESH,
        ).wait_recv()

    inputs = []
    idx_copy = pltpu.make_async_copy(idx_ref, idx_s, in_sem.at[3])
    for i, ref in enumerate((xq_ref, xp_ref, xh_ref)):
        copy = pltpu.make_async_copy(ref, xs.at[pl.ds(i * ROWS, ROWS)], in_sem.at[i])
        copy.start()
        inputs.append(copy)
    for k in range(MODEL // CHUNK):
        pltpu.make_async_copy(w_ref.at[pl.ds(k * CHUNK, CHUNK)], w.at[pl.ds(k * CHUNK, CHUNK)], w_sem.at[k]).start()

    idx_copy.start()

    barrier = pltpu.get_barrier_semaphore()

    def greet(k, carry):
        pl.semaphore_signal(barrier, inc=1, device_id=q_peer((q_slot + k) % 16), device_id_type=pl.DeviceIdType.MESH)
        pl.semaphore_signal(barrier, inc=1, device_id=p_peer((p_slot + k) % 16), device_id_type=pl.DeviceIdType.MESH)
        return carry

    lax.fori_loop(1, 16, greet, 0)

    for copy in inputs:
        copy.wait()
    acc[...] = jnp.zeros_like(acc)

    def project(k, carry):
        first = pl.multiple_of(k * CHUNK, CHUNK)
        pltpu.make_async_copy(w_ref.at[pl.ds(first, CHUNK)], w.at[pl.ds(first, CHUNK)], w_sem.at[k]).wait()
        acc[...] += jnp.dot(xs[:, pl.ds(first, CHUNK)], w[pl.ds(first, CHUNK), :], preferred_element_type=f32)
        return carry

    for k in range(MODEL // CHUNK):
        project(k, 0)

    def normalise(i):
        emb = acc[i * ROWS : (i + 1) * ROWS, :]
        s = lax.rsqrt(jnp.sum(emb * emb, axis=1, keepdims=True) + epsilon)
        u = emb * s
        scale[i * ROWS : (i + 1) * ROWS, :] = jnp.broadcast_to(s, (ROWS, 128))
        unit[i * ROWS : (i + 1) * ROWS, :] = u
        return u.astype(bf16)

    q_all[pl.ds(pl.multiple_of(q_slot * ROWS, ROWS), ROWS), :] = normalise(0)
    p_all[pl.ds(pl.multiple_of(p_slot * ROWS, ROWS), ROWS), :] = normalise(1)
    h_own[...] = normalise(2)
    pl.semaphore_wait(barrier, 30)

    def z_dev(v):
        return device(x, y, zmod(z + v), core)

    other = device(x, y, z, 1 - core)
    xl, xr, yl, yr = mod4(x + d), mod4(x - d), mod4(y + d), mod4(y - d)
    x2, y2 = mod4(x + 2), mod4(y + 2)
    to_xl, to_xr, to_x2 = device(xl, y, z, core), device(xr, y, z, core), device(x2, y, z, core)
    to_yl, to_yr, to_y2 = device(x, yl, z, core), device(x, yr, z, core), device(x, y2, z, core)

    def qz(zz, cc):
        return zmod(zz) * 2 + cc

    def push(ref, slot, to, first=0, count=ROWS):
        part = rows(ref, slot, first, count)
        return remote(part, part, to)

    def await_rows(n, ref, slot, first=0, count=ROWS):
        arrive(n, rows(ref, slot, first, count))

    other_in = []

    def share(v, first=0, count=ROWS):
        n = push(q_all, qz(z + v * d, core), other, first, count)
        other_in.append((n, qz(z - v * d, 1 - core), first, count))

    A, B = 0, HALF
    share(0)
    q2 = [[push(q_all, q_slot, z_dev(2 * d), hf * HALF, HALF), push(q_all, q_slot, z_dev(-2 * d), hf * HALF, HALF)] for hf in range(2)]
    p_from_xr = push(p_all, p_slot, to_xl)
    p_from_xl = push(p_all, p_slot, to_xr)
    p_from_yr = push(p_all, p_slot, to_yl)
    p_from_yl = push(p_all, p_slot, to_yr)
    p_from_x2 = push(p_all, p_slot, to_x2)
    p_from_y2 = push(p_all, p_slot, to_y2)
    q1l = push(q_all, q_slot, z_dev(d))
    q1s = push(q_all, q_slot, z_dev(-d))

    def column(m):
        return m // 2, m % 2

    relay_dev = (pb, y_hi * 16 + zmod(z + d * pb) * 2 + core)
    src_z = zmod(z - d * pb)
    src_dev = (pb, y_hi * 16 + src_z * 2 + core)
    goal_pb, goal_hi = column(y_hi * 8 + src_z)
    goal_dev = (goal_pb, goal_hi * 16 + q_slot)
    mine = 2 * pb + y_hi
    from_hi, from_z = mine // 8, mine % 8
    from_pb = zmod(d * (z - from_z))
    from_dev = (from_pb, from_hi * 16 + q_slot)
    relays_self = pb == 0
    goal_self = jnp.logical_and(goal_pb == pb, goal_hi == y_hi)
    from_self = jnp.logical_and(from_pb == pb, from_hi == y_hi)

    def hop(k, src, dst, to):
        return pltpu.make_async_remote_copy(
            src_ref=src, dst_ref=dst, send_sem=hop_sem.at[2 * k], recv_sem=hop_sem.at[2 * k + 1],
            device_id=to, device_id_type=pl.DeviceIdType.MESH,
        )

    def hop_start(k, src, dst, to, is_self):
        @pl.when(jnp.logical_not(is_self))
        def _():
            hop(k, src, dst, to).start()

        @pl.when(is_self)
        def _():
            dst[...] = src[...]

    def hop_recv(k, src, dst, to, is_self):
        @pl.when(jnp.logical_not(is_self))
        def _():
            hop(k, src, dst, to).wait_recv()

    def hop_sent(k, src, dst, to, is_self):
        @pl.when(jnp.logical_not(is_self))
        def _():
            hop(k, src, dst, to).wait_send()

    h1 = (0, h_own, h_rel, relay_dev, relays_self)
    h2 = (1, h_rel, h_in, goal_dev, goal_self)
    h3 = (2, dh_out, dh_rel, from_dev, from_self)
    h4 = (3, dh_rel, dh_in, src_dev, relays_self)

    await_rows(p_from_xr, p_all, slot_of(xr, y))
    n_xr_yl = push(p_all, slot_of(xr, y), to_yl, A, HALF)
    n_xr_yr = push(p_all, slot_of(xr, y), to_yr, A, HALF)
    await_rows(p_from_yr, p_all, slot_of(x, yr))
    m_yr_xl = push(p_all, slot_of(x, yr), to_xl, B, HALF)
    m_yr_xr = push(p_all, slot_of(x, yr), to_xr, B, HALF)
    await_rows(p_from_xl, p_all, slot_of(xl, y))
    n_xl_yl = push(p_all, slot_of(xl, y), to_yl, A, HALF)
    n_xl_yr = push(p_all, slot_of(xl, y), to_yr, A, HALF)
    await_rows(p_from_yl, p_all, slot_of(x, yl))
    m_yl_xl = push(p_all, slot_of(x, yl), to_xl, B, HALF)
    m_yl_xr = push(p_all, slot_of(x, yl), to_xr, B, HALF)
    q4, q3l, q3s = [], [], []
    for hf in range(2):
        f = hf * HALF
        await_rows(q2[hf][0], q_all, qz(z - 2 * d, core), f, HALF)
        share(-2, f, HALF)
        q4.append(push(q_all, qz(z - 2 * d, core), z_dev(2 * d), f, HALF))
        q3l.append(push(q_all, qz(z - 2 * d, core), z_dev(d), f, HALF))
        await_rows(q2[hf][1], q_all, qz(z + 2 * d, core), f, HALF)
        share(2, f, HALF)
        q3s.append(push(q_all, qz(z + 2 * d, core), z_dev(-d), f, HALF))
    hop_start(*h1)
    await_rows(q1l, q_all, qz(z - d, core))
    share(-1)
    await_rows(q1s, q_all, qz(z + d, core))
    share(1)
    await_rows(p_from_x2, p_all, slot_of(x2, y))
    n_x2_y2 = push(p_all, slot_of(x2, y), to_y2, A, HALF)
    n_x2_yl = push(p_all, slot_of(x2, y), to_yl, A, HALF)
    n_x2_yr = push(p_all, slot_of(x2, y), to_yr, A, HALF)
    await_rows(p_from_y2, p_all, slot_of(x, y2))
    m_y2_x2 = push(p_all, slot_of(x, y2), to_x2, B, HALF)
    m_y2_xl = push(p_all, slot_of(x, y2), to_xl, B, HALF)
    m_y2_xr = push(p_all, slot_of(x, y2), to_xr, B, HALF)
    await_rows(n_xr_yl, p_all, slot_of(xr, yr), A, HALF)
    k_xr = push(p_all, slot_of(xr, yr), to_yl, A, HALF)
    await_rows(m_yr_xl, p_all, slot_of(xr, yr), B, HALF)
    l_yr = push(p_all, slot_of(xr, yr), to_xl, B, HALF)
    await_rows(n_xl_yl, p_all, slot_of(xl, yr), A, HALF)
    k_xl = push(p_all, slot_of(xl, yr), to_yl, A, HALF)
    await_rows(m_yl_xl, p_all, slot_of(xr, yl), B, HALF)
    l_yl = push(p_all, slot_of(xr, yl), to_xl, B, HALF)
    for hf in range(2):
        f = hf * HALF
        await_rows(q3s[hf], q_all, qz(z + 3 * d, core), f, HALF)
        share(3, f, HALF)
        await_rows(q3l[hf], q_all, qz(z - 3 * d, core), f, HALF)
        share(-3, f, HALF)
    for hf in range(2):
        f = hf * HALF
        await_rows(q4[hf], q_all, qz(z + 4, core), f, HALF)
        share(4, f, HALF)
    await_rows(n_xr_yr, p_all, slot_of(xr, yl), A, HALF)
    await_rows(n_xl_yr, p_all, slot_of(xl, yl), A, HALF)
    await_rows(m_yr_xr, p_all, slot_of(xl, yr), B, HALF)
    await_rows(m_yl_xr, p_all, slot_of(xl, yl), B, HALF)
    await_rows(n_x2_y2, p_all, slot_of(x2, y2), A, HALF)
    await_rows(m_y2_x2, p_all, slot_of(x2, y2), B, HALF)
    await_rows(n_x2_yl, p_all, slot_of(x2, yr), A, HALF)
    await_rows(m_y2_xl, p_all, slot_of(xr, y2), B, HALF)
    await_rows(n_x2_yr, p_all, slot_of(x2, yl), A, HALF)
    await_rows(m_y2_xr, p_all, slot_of(xl, y2), B, HALF)
    await_rows(k_xr, p_all, slot_of(xr, y2), A, HALF)
    await_rows(k_xl, p_all, slot_of(xl, y2), A, HALF)
    await_rows(l_yr, p_all, slot_of(x2, yr), B, HALF)
    await_rows(l_yl, p_all, slot_of(x2, yl), B, HALF)
    for n, slot, first, count in other_in:
        await_rows(n, q_all, slot, first, count)

    hop_recv(*h1)
    hop_start(*h2)

    csum[...] = jnp.zeros_like(csum)

    def score(t, carry):
        first = pl.multiple_of(t * TILE, TILE)
        s = nt(q_all[pl.ds(first, TILE), :], p_all[...])
        e = jnp.exp(inverse_temp * s - inverse_temp)
        e_s[pl.ds(first, TILE), :] = e
        csum[...] += jnp.sum(e.reshape(TILE // 8, 8, GROUP), axis=0)
        part = e[:, :128]
        for j in range(1, GROUP // 128):
            part = part + e[:, j * 128 : (j + 1) * 128]
        for j in range(TILE // 128):
            row = jnp.sum(jnp.transpose(part[j * 128 : (j + 1) * 128, :]), axis=0, keepdims=True)
            tq[q_slot, pl.ds(t * (TILE // 128) + j, 1), :] = row
        return carry

    for t in range(GROUP // TILE):
        score(t, 0)
    total = jnp.sum(csum[...], axis=0, keepdims=True)
    for j in range(GROUP // 128):
        tp[p_slot, pl.ds(j, 1), :] = total[:, j * 128 : (j + 1) * 128]

    hop_recv(*h2)
    q_half = pl.ds(pl.multiple_of(core * 512, 512), 512)
    idx_copy.wait()
    hidx = idx_s[y_hi * 2 + core] - (from_hi * 16 + q_slot_of(from_z)) * 512 - from_pb * ROWS
    hidx = jnp.concatenate([hidx[j : j + 1, :] for j in range(4)], axis=1)
    named = lax.broadcasted_iota(jnp.int32, (ROWS, 512), 0) == hidx
    e_hard = jnp.exp(inverse_temp * nt(h_in[...], q_all[q_half, :]) - inverse_temp)
    e_hard = jnp.where(named, e_hard, 0.0)
    eh[...] = e_hard
    hard_sum = jnp.sum(e_hard, axis=0, keepdims=True)
    for j in range(4):
        tq[q_slot, pl.ds(core * 4 + j, 1), :] += hard_sum[:, j * 128 : (j + 1) * 128]

    eye = lax.broadcasted_iota(jnp.int32, (128, 128), 0) == lax.broadcasted_iota(jnp.int32, (128, 128), 1)

    def tell(k, carry):
        pltpu.make_async_remote_copy(
            src_ref=tq.at[q_slot], dst_ref=tq.at[q_slot], send_sem=tq_send.at[k], recv_sem=tq_recv.at[q_slot],
            device_id=q_peer((q_slot + k) % 16), device_id_type=pl.DeviceIdType.MESH,
        ).start()
        pltpu.make_async_remote_copy(
            src_ref=tp.at[p_slot], dst_ref=tp.at[p_slot], send_sem=tp_send.at[k], recv_sem=tp_recv.at[p_slot],
            device_id=p_peer((p_slot + k) % 16), device_id_type=pl.DeviceIdType.MESH,
        ).start()
        return carry

    def heard(k, carry):
        sq, sp = (q_slot + k) % 16, (p_slot + k) % 16
        pltpu.make_async_remote_copy(
            src_ref=tq.at[q_slot], dst_ref=tq.at[sq], send_sem=tq_send.at[k], recv_sem=tq_recv.at[sq],
            device_id=(pb, pa), device_id_type=pl.DeviceIdType.MESH,
        ).wait()
        pltpu.make_async_remote_copy(
            src_ref=tp.at[p_slot], dst_ref=tp.at[sp], send_sem=tp_send.at[k], recv_sem=tp_recv.at[sp],
            device_id=(pb, pa), device_id_type=pl.DeviceIdType.MESH,
        ).wait()
        return carry

    for k in range(1, 16):
        tell(k, 0)

    is_keeper = z == mine % 8
    kb = mine // 8
    ka = core

    @pl.when(is_keeper)
    def _():
        for j in range(4):
            q_rows = q_all[pl.ds(pl.multiple_of(ka * 512 + j * 128, 128), 128), :]
            p_rows = p_all[pl.ds(pl.multiple_of(kb * 512 + j * 128, 128), 128), :]
            diag = jnp.where(eye, inverse_temp * nt(q_rows, p_rows), 0.0)
            dg[j : j + 1, :] = jnp.sum(diag, axis=0, keepdims=True)

    def diag_copy(k, dst, to, at):
        return pltpu.make_async_remote_copy(
            src_ref=dg, dst_ref=dst, send_sem=dg_send.at[k], recv_sem=dg_recv.at[at],
            device_id=to, device_id_type=pl.DeviceIdType.MESH,
        )

    def keep(act):
        @pl.when(is_keeper)
        def _():
            for k in range(8):
                sq, sp = ka * 8 + k, kb * 8 + k

                @pl.when(sq != q_slot)
                def _():
                    act(diag_copy(k, dgq, q_peer(sq), 0))

                @pl.when(sp != p_slot)
                def _():
                    act(diag_copy(8 + k, dgp, p_peer(sp), 1))

    keep(lambda copy: copy.start())
    dgq_self = jnp.logical_and(is_keeper, q_slot // 8 == ka)
    dgp_self = jnp.logical_and(is_keeper, p_slot // 8 == kb)

    @pl.when(dgq_self)
    def _():
        dgq[...] = dg[...]

    @pl.when(dgp_self)
    def _():
        dgp[...] = dg[...]

    def turn(k, carry):
        first = pl.multiple_of(k * CHUNK, CHUNK)
        wt[:, pl.ds(first, CHUNK)] = jnp.transpose(w[pl.ds(first, CHUNK), :])
        return carry

    lax.fori_loop(0, MODEL // CHUNK, turn, 0)
    for k in range(1, 16):
        heard(k, 0)
    sq = jnp.sum(tq[...], axis=0)
    sp = jnp.sum(tp[...], axis=0)
    rinv = inverse_temp / sq
    cinv = inverse_temp / sp
    rin_s[...] = rinv
    lrow_s[0:8, :] = sq
    lrow_s[8:16, :] = sp

    hard_weight = jnp.concatenate([rin_s[pl.ds(core * 4 + j, 1), :] for j in range(4)], axis=1)
    gh[...] = (eh[...] * hard_weight).astype(bf16)
    dh_out[...] = jnp.dot(gh[...], q_all[q_half, :], preferred_element_type=f32).astype(bf16)
    hop_start(*h3)
    for j in range(8):
        rcol[j * 128 : (j + 1) * 128, :] = jnp.transpose(jnp.broadcast_to(rinv[j : j + 1, :], (128, 128)))
        crow[:, j * 128 : (j + 1) * 128] = jnp.broadcast_to(cinv[j : j + 1, :], (8, 128))
    tile_s[...] = tn(gh[...], h_in[...])

    @pl.when(is_keeper)
    def _():
        for j in range(4):
            r = pl.multiple_of(ka * 512 + j * 128, 128)
            c = pl.multiple_of(kb * 512 + j * 128, 128)
            factor = rcol[pl.ds(r, 128), :] + crow[0:1, pl.ds(c, 128)]
            e_s[pl.ds(r, 128), pl.ds(c, 128)] -= jnp.where(eye, 2.0 * inverse_temp / factor, 0.0)

    t0 = zmod(z + 4) // 2

    def question_tile(i, carry):
        t = (t0 + i) % 4
        first = pl.multiple_of(t * TILE, TILE)
        factor = wide(rcol[pl.ds(first, TILE), :], GROUP // 128) + crow[0:1, :]
        weights = (e_s[pl.ds(first, TILE), :] * factor).astype(bf16)
        g_s[pl.ds(first, TILE), :] = weights
        value = jnp.dot(weights, p_all[...], preferred_element_type=f32)
        here = (t // 2 == core).astype(f32)
        value = value + here * tile_s[pl.ds(pl.multiple_of((t % 2) * TILE, TILE), TILE), :]
        for j in range(4):
            dq[j % 2, t * 2 + j // 2] = value[j * ROWS : (j + 1) * ROWS, :].astype(bf16)
        pltpu.make_async_remote_copy(
            src_ref=dq.at[1 - core, pl.ds(t * 2, 2)], dst_ref=prt.at[pl.ds(t * 2, 2)],
            send_sem=pt_send.at[t], recv_sem=pt_recv.at[t],
            device_id=other, device_id_type=pl.DeviceIdType.MESH,
        ).start()
        return carry

    for i in range(4):
        question_tile(i, 0)

    def passage_tile(t, carry):
        first = pl.multiple_of(t * TILE, TILE)
        value = tn(g_s[:, pl.ds(first, TILE)], q_all[...]).astype(bf16)
        for j in range(4):
            slot = t * 4 + j
            yy = (slot // 8) * 2 + j % 2
            xx = (slot % 8) // 2
            dpa[yy, xx] = value[j * ROWS : j * ROWS + HALF, :]
            dpb[xx, yy] = value[j * ROWS + HALF : (j + 1) * ROWS, :]
        return carry

    for t in range(2):
        passage_tile(t, 0)

    def own_sum(k, carry):
        t = k
        pltpu.make_async_remote_copy(
            src_ref=dq.at[1 - core, pl.ds(t * 2, 2)], dst_ref=prt.at[pl.ds(t * 2, 2)],
            send_sem=pt_send.at[t], recv_sem=pt_recv.at[t],
            device_id=other, device_id_type=pl.DeviceIdType.MESH,
        ).wait()
        prt[pl.ds(t * 2, 2)] = (
            prt[pl.ds(t * 2, 2)].astype(f32) + dq[core, pl.ds(t * 2, 2)].astype(f32)
        ).astype(bf16)
        return carry

    for i in range(4):
        own_sum((t0 + i) % 4, 0)

    def half(ref, hf):
        return ref.at[pl.ds(hf * HALF, HALF)]

    r4, r3l, r3s = [], [], []
    for hf in range(2):
        r4.append(remote(half(prt.at[zmod(z + 4)], hf), half(zr.at[0], hf), z_dev(-2 * d)))
        r3l.append(remote(half(prt.at[zmod(z - 3 * d)], hf), half(zr.at[1], hf), z_dev(-d)))
        r3s.append(remote(half(prt.at[zmod(z + 3 * d)], hf), half(zr.at[2], hf), z_dev(d)))
    r1l = remote(prt.at[zmod(z - d)], zin.at[0], z_dev(-d))
    r1s = remote(prt.at[zmod(z + d)], zin.at[1], z_dev(d))

    for t in range(2, 4):
        passage_tile(t, 0)

    def pair(ref, i):
        return ref.at[pl.ds(i * 2, 2)]

    n_a1 = [remote(pair(dpa.at[y2], i), pair(a1.at[0], i), to_yr) for i in range(2)]
    n_b1 = [remote(pair(dpb.at[x2], i), pair(b1.at[0], i), to_xr) for i in range(2)]
    n_a1s = remote(dpa.at[yl], a1.at[1], to_yl)
    n_b1s = remote(dpb.at[xl], b1.at[1], to_xl)

    n_a1l, n_b1l = [], []
    for i in range(2):
        two = slice(i * 2, i * 2 + 2)
        arrive(n_a1[i], pair(a1.at[0], i))
        a1[0, two] = (a1[0, two].astype(f32) + dpa[yr, two].astype(f32)).astype(bf16)
        n_a1l.append(remote(pair(a1.at[0], i), pair(a1.at[2], i), to_yr))
        arrive(n_b1[i], pair(b1.at[0], i))
        b1[0, two] = (b1[0, two].astype(f32) + dpb[xr, two].astype(f32)).astype(bf16)
        n_b1l.append(remote(pair(b1.at[0], i), pair(b1.at[2], i), to_xr))

    r2l, r2s = [], []
    for hf in range(2):
        part = slice(hf * HALF, (hf + 1) * HALF)
        arrive(r3s[hf], half(zr.at[2], hf))
        zr[2, part, :] = (zr[2, part, :].astype(f32) + prt[zmod(z + 2 * d), part, :].astype(f32)).astype(bf16)
        r2s.append(remote(half(zr.at[2], hf), half(zin.at[3], hf), z_dev(2 * d)))
        arrive(r3l[hf], half(zr.at[1], hf))
        arrive(r4[hf], half(zr.at[0], hf))
        zr[1, part, :] = (
            zr[1, part, :].astype(f32) + zr[0, part, :].astype(f32) + prt[zmod(z - 2 * d), part, :].astype(f32)
        ).astype(bf16)
        r2l.append(remote(half(zr.at[1], hf), half(zin.at[2], hf), z_dev(-2 * d)))

    hop_recv(*h3)
    hop_start(*h4)

    arrive(n_a1s, a1.at[1])
    for i in range(2):
        arrive(n_a1l[i], pair(a1.at[2], i))
    a1[1] = (a1[1].astype(f32) + a1[2].astype(f32) + dpa[y].astype(f32)).astype(bf16)
    n_a2 = [remote(a1.at[1, xx], a2.at[i], to) for i, (xx, to) in enumerate(((x2, to_x2), (xl, to_xl), (xr, to_xr)))]
    arrive(n_b1s, b1.at[1])
    for i in range(2):
        arrive(n_b1l[i], pair(b1.at[2], i))
    b1[1] = (b1[1].astype(f32) + b1[2].astype(f32) + dpb[x].astype(f32)).astype(bf16)
    n_b2 = [remote(b1.at[1, yy], b2.at[i], to) for i, (yy, to) in enumerate(((y2, to_y2), (yl, to_yl), (yr, to_yr)))]

    def back(grad, i, first, count):
        part = slice(i * ROWS + first, i * ROWS + first + count)
        u = unit[part, :]
        along = jnp.sum(grad * u, axis=1, keepdims=True)
        ge[part, :] = ((grad - u * along) * wide(scale[part, :], WIDTH // 128)).astype(bf16)

    keeper_q = mine % 8
    group_p = y_hi * 8 + z

    @pl.when(jnp.logical_not(dgq_self))
    def _():
        diag_copy(0, dgq, (pb, y_hi * 16 + keeper_q * 2 + z // 4), 0).wait_recv()

    @pl.when(jnp.logical_not(dgp_self))
    def _():
        diag_copy(0, dgp, (group_p // 2, (group_p % 2) * 16 + q_slot), 1).wait_recv()

    def loss(total_row, diag, first):
        value = inverse_temp + jnp.log(total_row) - diag
        return jnp.where(first, value[:, :ROWS], value[:, ROWS:])

    loss_s[0, 0:1, 0:ROWS] = loss(lrow_s[pl.ds(z, 1), :], dgq[pl.ds(z % 4, 1), :], core == 0)
    loss_s[1, 0:1, 0:ROWS] = loss(lrow_s[pl.ds(8 + y_hi * 4 + x, 1), :], dgp[pl.ds(x, 1), :], y_lo == 0)
    loss_copies = [pltpu.make_async_copy(loss_s.at[i], ref, o_sem.at[3, i]) for i, ref in enumerate((lq_ref, lp_ref))]
    for copy in loss_copies:
        copy.start()

    hop_recv(*h4)
    back(dh_in[...].astype(f32), 2, 0, ROWS)

    arrive(r1l, zin.at[0])
    arrive(r1s, zin.at[1])
    for hf in range(2):
        arrive(r2s[hf], half(zin.at[3], hf))
        arrive(r2l[hf], half(zin.at[2], hf))
    back(jnp.sum(zin[...].astype(f32), axis=0) + prt[z].astype(f32), 0, 0, ROWS)
    for i in range(3):
        arrive(n_a2[i], a2.at[i])
    back(jnp.sum(a2[...].astype(f32), axis=0) + a1[1, x].astype(f32), 1, 0, HALF)
    for i in range(3):
        arrive(n_b2[i], b2.at[i])
    back(jnp.sum(b2[...].astype(f32), axis=0) + b1[1, y].astype(f32), 1, HALF, HALF)

    def out_copies(k):
        columns = pl.ds(pl.multiple_of(k * CHUNK, CHUNK), CHUNK)
        return [
            pltpu.make_async_copy(out_s.at[pl.ds(i * ROWS, ROWS), columns], ref.at[:, columns], o_sem.at[i, k])
            for i, ref in enumerate((oq_ref, op_ref, oh_ref))
        ]

    def unproject(k, carry):
        first = pl.multiple_of(k * CHUNK, CHUNK)
        out_s[:, pl.ds(first, CHUNK)] = jnp.dot(
            ge[...], wt[:, pl.ds(first, CHUNK)], preferred_element_type=f32
        ).astype(bf16)
        for copy in out_copies(k):
            copy.start()
        return carry

    for k in range(MODEL // CHUNK):
        unproject(k, 0)

    for copy in started:
        copy.wait_send()
    for h in (h1, h2, h3, h4):
        hop_sent(*h)
    keep(lambda copy: copy.wait_send())
    for k in range(MODEL // CHUNK):
        for copy in out_copies(k):
            copy.wait()
    for copy in loss_copies:
        copy.wait()


def hand_on(gq, gp, gh, lq, lp, oq, op, oh, olq, olp, stage, lstage, lflat, in_sem, out_sem):
    arrivals = [pltpu.make_async_copy(src, stage.at[i], in_sem.at[i]) for i, src in enumerate((gq, gp, gh))]
    losses = [pltpu.make_async_copy(src, lstage.at[i], in_sem.at[3 + i]) for i, src in enumerate((lq, lp))]
    leaving = [pltpu.make_async_copy(stage.at[i], dst, out_sem.at[i]) for i, dst in enumerate((oq, op, oh))]
    leaving += [pltpu.make_async_copy(lflat.at[i], dst, out_sem.at[3 + i]) for i, dst in enumerate((olq, olp))]
    for copy in losses + arrivals:
        copy.start()
    for i, copy in enumerate(losses):
        copy.wait()
        lflat[i, :] = lstage[i, 0, 0:ROWS]
        leaving[3 + i].start()
    for i, copy in enumerate(arrivals):
        copy.wait()
        leaving[i].start()
    for copy in leaving:
        copy.wait()


COPIES = 120


def shards(questions, passages, hard_rows, hard_index, projection):
    vmem = pl.BlockSpec(memory_space=pltpu.VMEM)
    hbm = pl.BlockSpec(memory_space=pl.ANY)
    out = jax.ShapeDtypeStruct((ROWS, MODEL), bf16)
    loss = jax.ShapeDtypeStruct((8, 128), f32)
    flat = jax.ShapeDtypeStruct((ROWS,), f32)
    V, D = pltpu.VMEM, pltpu.SemaphoreType.DMA
    gq, gp, gh, lq, lp = pl.pallas_call(
        kernel,
        out_shape=(out, out, out, loss, loss),
        in_specs=[hbm] * 5,
        out_specs=(hbm,) * 5,
        scratch_shapes=[
            V((3 * ROWS, MODEL), bf16),
            V((MODEL, WIDTH), bf16),
            V((WIDTH, MODEL), bf16),
            V((3 * ROWS, WIDTH), f32),
            V((3 * ROWS, WIDTH), f32),
            V((3 * ROWS, 128), f32),
            V((GROUP, WIDTH), bf16),
            V((GROUP, WIDTH), bf16),
            V((ROWS, WIDTH), bf16),
            V((ROWS, WIDTH), bf16),
            V((ROWS, WIDTH), bf16),
            V((ROWS, WIDTH), bf16),
            V((ROWS, WIDTH), bf16),
            V((ROWS, WIDTH), bf16),
            V((ROWS, 512), f32),
            V((ROWS, 512), bf16),
            V((GROUP, GROUP), f32),
            V((GROUP, GROUP), bf16),
            V((512, WIDTH), f32),
            V((8, GROUP), f32),
            V((16, 8, 128), f32),
            V((16, 8, 128), f32),
            V((GROUP, 128), f32),
            V((8, GROUP), f32),
            V((8, 128), f32),
            V((8, 128), f32),
            V((8, 128), f32),
            V((8, 128), f32),
            V((16, 128), f32),
            V((2, 8, ROWS, WIDTH), bf16),
            V((8, ROWS, WIDTH), bf16),
            V((3, ROWS, WIDTH), bf16),
            V((4, ROWS, WIDTH), bf16),
            V((4, 4, HALF, WIDTH), bf16),
            V((4, 4, HALF, WIDTH), bf16),
            V((3, 4, HALF, WIDTH), bf16),
            V((3, 4, HALF, WIDTH), bf16),
            V((3, HALF, WIDTH), bf16),
            V((3, HALF, WIDTH), bf16),
            V((3 * ROWS, WIDTH), bf16),
            V((3 * ROWS, MODEL), bf16),
            V((4, 4, 128), jnp.int32),
            V((2, 8, 128), f32),
            D((4,)), D((MODEL // CHUNK,)),
            D((COPIES,)), D((COPIES,)),
            D((16,)), D((16,)), D((16,)), D((16,)),
            D((16,)), D((2,)), D((8,)), D((4,)), D((4,)), D((4, MODEL // CHUNK)),
        ],
        compiler_params=pltpu.CompilerParams(
            collective_id=0, has_side_effects=True, vmem_limit_bytes=56 * 1024 * 1024
        ),
        cost_estimate=pl.CostEstimate(flops=8 * 10**9, bytes_accessed=10**7, transcendentals=10**6),
    )(questions, passages, hard_rows, hard_index.reshape(4, 4, 128), projection)
    return pl.pallas_call(
        hand_on,
        out_shape=(out, out, out, flat, flat),
        in_specs=(hbm,) * 5,
        out_specs=(hbm,) * 5,
        scratch_shapes=[V((3, ROWS, MODEL), bf16), V((2, 8, 128), f32), V((2, ROWS), f32), D((5,)), D((5,))],
        compiler_params=pltpu.CompilerParams(vmem_limit_bytes=56 * 1024 * 1024),
        cost_estimate=pl.CostEstimate(flops=0, bytes_accessed=3 * 10**6, transcendentals=0),
    )(gq, gp, gh, lq, lp)


def solution(mesh):
    in_specs = (P(("pb", "pa"), None), P(("pa", "pb"), None), P(("pa", "pb"), None), P("pb"), P())
    out_specs = (
        P(("pb", "pa"), None),
        P(("pa", "pb"), None),
        P(("pa", "pb"), None),
        P(("pb", "pa")),
        P(("pa", "pb")),
    )
    return jax.shard_map(shards, mesh=mesh, in_specs=in_specs, out_specs=out_specs, check_vma=False)
```

```python
import math

import jax
import jax.numpy as jnp
from jax import lax
from jax.experimental import pallas as pl
from jax.experimental.pallas import tpu as pltpu
from jax.sharding import PartitionSpec as P

inverse_temp = 40.0
epsilon = 1e-06
f32 = jnp.float32
bf16 = jnp.bfloat16

NZ, NX, NY = 8, 4, 4
ROWS = 64
HALF = 32
GROUP = 1024
WIDTH = 768
MODEL = 4096
CHUNK = 1024
TILE = 256


def nt(a, b):
    return lax.dot_general(a, b, (((1,), (1,)), ((), ())), preferred_element_type=f32)


def tn(a, b):
    return lax.dot_general(a, b, (((0,), (0,)), ((), ())), preferred_element_type=f32)


def wide(column, times):
    return jnp.concatenate([column] * times, axis=1)


def kernel(
    xq_ref, xp_ref, xh_ref, idx_ref, w_ref,
    oq_ref, op_ref, oh_ref, lq_ref, lp_ref,
    xs, w, wt, acc, unit, scale, q_all, p_all, h_own, h_rel, h_in, dh_out, dh_rel, dh_in, hw_out, hw_rel, hw_in, eh, gh,
    e_s, g_s, tile_s, csum, tq, tp, rcol, crow, rin_s, dg, dgq, dgp, lrow_s,
    dq, prt, zr, zin, dpa, dpb, a1, b1, a2, b2, ge, out_s,
    idx_s, loss_s,
    in_sem, w_sem, send, recv, t_sem, dg_send, dg_recv, hop_sem, o_sem,
):
    pb, pa = lax.axis_index("pb"), lax.axis_index("pa")
    x, y_lo = pb // 2, pb % 2
    y_hi, z, core = pa // 16, (pa // 2) % 8, pa % 2
    y = y_hi * 2 + y_lo
    d = 1 - 2 * core

    def device(xx, yy, zz, cc):
        return (xx * 2 + yy % 2, (yy // 2) * 16 + zz * 2 + cc)

    def zmod(v):
        return (v + 16) % 8

    def mod4(v):
        return (v + 8) % 4

    q_slot = core * 8 + z
    p_slot = y * 4 + x
    zc = z * 2 + core

    def q_slot_of(zz):
        return zz * 2 + core

    def q_peer(s):
        return (pb, y_hi * 16 + (s % 8) * 2 + s // 8)

    def p_peer(s):
        return device(s % 4, s // 4, z, core)

    def slot_of(xx, yy):
        return yy * 4 + xx

    def rows(ref, slot, first=0, count=ROWS):
        return ref.at[pl.ds(pl.multiple_of(slot * ROWS + first, HALF), count)]

    counter = [0]
    phase = [0]
    sent_rows = [0, 0]

    def remote(src, dst, to, at=None):
        n = counter[0] if at is None else at
        if at is None:
            counter[0] += 1
        sent_rows[phase[0]] += math.prod(src.shape) // WIDTH
        pltpu.make_async_remote_copy(
            src_ref=src, dst_ref=dst, send_sem=send.at[phase[0]], recv_sem=recv.at[n],
            device_id=to, device_id_type=pl.DeviceIdType.MESH,
        ).start()
        return n

    def arrive(n, dst):
        pltpu.make_async_remote_copy(
            src_ref=dst, dst_ref=dst, send_sem=send.at[0], recv_sem=recv.at[n],
            device_id=(pb, pa), device_id_type=pl.DeviceIdType.MESH,
        ).wait_recv()

    def all_sent(i):
        part = w.at[pl.ds(0, sent_rows[i])]
        pltpu.make_async_remote_copy(
            src_ref=part, dst_ref=part, send_sem=send.at[i], recv_sem=recv.at[0],
            device_id=(pb, pa), device_id_type=pl.DeviceIdType.MESH,
        ).wait_send()

    inputs = []
    idx_copy = pltpu.make_async_copy(idx_ref, idx_s, in_sem.at[3])
    for i, ref in enumerate((xq_ref, xp_ref, xh_ref)):
        copy = pltpu.make_async_copy(ref, xs.at[pl.ds(i * ROWS, ROWS)], in_sem.at[i])
        copy.start()
        inputs.append(copy)
    for k in range(MODEL // CHUNK):
        pltpu.make_async_copy(w_ref.at[pl.ds(k * CHUNK, CHUNK)], w.at[pl.ds(k * CHUNK, CHUNK)], w_sem.at[k]).start()

    idx_copy.start()

    barrier = pltpu.get_barrier_semaphore()

    def greet(k, carry):
        pl.semaphore_signal(barrier, inc=1, device_id=q_peer((q_slot + k) % 16), device_id_type=pl.DeviceIdType.MESH)
        pl.semaphore_signal(barrier, inc=1, device_id=p_peer((p_slot + k) % 16), device_id_type=pl.DeviceIdType.MESH)
        return carry

    lax.fori_loop(1, 16, greet, 0)

    for copy in inputs:
        copy.wait()
    acc[...] = jnp.zeros_like(acc)

    def project(k, carry):
        first = pl.multiple_of(k * CHUNK, CHUNK)
        pltpu.make_async_copy(w_ref.at[pl.ds(first, CHUNK)], w.at[pl.ds(first, CHUNK)], w_sem.at[k]).wait()
        acc[...] += jnp.dot(xs[:, pl.ds(first, CHUNK)], w[pl.ds(first, CHUNK), :], preferred_element_type=f32)
        return carry

    for k in range(MODEL // CHUNK):
        project(k, 0)

    def normalise(i):
        emb = acc[i * ROWS : (i + 1) * ROWS, :]
        s = lax.rsqrt(jnp.sum(emb * emb, axis=1, keepdims=True) + epsilon)
        u = emb * s
        scale[i * ROWS : (i + 1) * ROWS, :] = jnp.broadcast_to(s, (ROWS, 128))
        unit[i * ROWS : (i + 1) * ROWS, :] = u
        return u.astype(bf16)

    q_all[pl.ds(pl.multiple_of(q_slot * ROWS, ROWS), ROWS), :] = normalise(0)
    p_all[pl.ds(pl.multiple_of(p_slot * ROWS, ROWS), ROWS), :] = normalise(1)
    h_own[...] = normalise(2)
    pl.semaphore_wait(barrier, 30)

    def z_dev(v):
        return device(x, y, zmod(z + v), core)

    other = device(x, y, z, 1 - core)
    xl, xr, yl, yr = mod4(x + d), mod4(x - d), mod4(y + d), mod4(y - d)
    x2, y2 = mod4(x + 2), mod4(y + 2)
    to_xl, to_xr, to_x2 = device(xl, y, z, core), device(xr, y, z, core), device(x2, y, z, core)
    to_yl, to_yr, to_y2 = device(x, yl, z, core), device(x, yr, z, core), device(x, y2, z, core)

    def qz(zz, cc):
        return cc * 8 + zmod(zz)

    def push(ref, slot, to, first=0, count=ROWS, at=None):
        part = rows(ref, slot, first, count)
        return remote(part, part, to, at)

    def await_rows(n, ref, slot, first=0, count=ROWS):
        arrive(n, rows(ref, slot, first, count))

    SHARED, LAST = COPIES - 1, COPIES - 2

    def share(v, first=0, count=ROWS):
        push(q_all, qz(z + v * d, core), other, first, count, SHARED)

    A, B = 0, HALF
    share(0)
    q2 = [[push(q_all, q_slot, z_dev(2 * d), hf * HALF, HALF), push(q_all, q_slot, z_dev(-2 * d), hf * HALF, HALF)] for hf in range(2)]
    p_from_xr = push(p_all, p_slot, to_xl)
    p_from_xl = push(p_all, p_slot, to_xr)
    p_from_yr = push(p_all, p_slot, to_yl)
    p_from_yl = push(p_all, p_slot, to_yr)
    p_from_x2 = push(p_all, p_slot, to_x2)
    p_from_y2 = push(p_all, p_slot, to_y2)
    q1l = push(q_all, q_slot, z_dev(d))
    q1s = push(q_all, q_slot, z_dev(-d))

    def column(m):
        return m // 2, m % 2

    relay_dev = (pb, y_hi * 16 + zmod(z + d * pb) * 2 + core)
    src_z = zmod(z - d * pb)
    src_dev = (pb, y_hi * 16 + src_z * 2 + core)
    goal_pb, goal_hi = column(y_hi * 8 + src_z)
    goal_dev = (goal_pb, goal_hi * 16 + zc)
    mine = 2 * pb + y_hi
    from_hi, from_z = mine // 8, mine % 8
    from_pb = zmod(d * (z - from_z))
    from_dev = (from_pb, from_hi * 16 + zc)
    relays_self = pb == 0
    goal_self = jnp.logical_and(goal_pb == pb, goal_hi == y_hi)
    from_self = jnp.logical_and(from_pb == pb, from_hi == y_hi)

    def hop(k, src, dst, to):
        return pltpu.make_async_remote_copy(
            src_ref=src, dst_ref=dst, send_sem=hop_sem.at[2 * k], recv_sem=hop_sem.at[2 * k + 1],
            device_id=to, device_id_type=pl.DeviceIdType.MESH,
        )

    def hop_start(k, src, dst, to, is_self):
        @pl.when(jnp.logical_not(is_self))
        def _():
            hop(k, src, dst, to).start()

        @pl.when(is_self)
        def _():
            dst[...] = src[...]

    def hop_recv(k, src, dst, to, is_self):
        @pl.when(jnp.logical_not(is_self))
        def _():
            hop(k, src, dst, to).wait_recv()

    def hop_sent(k, src, dst, to, is_self):
        @pl.when(jnp.logical_not(is_self))
        def _():
            hop(k, src, dst, to).wait_send()

    h1 = (0, h_own, h_rel, relay_dev, relays_self)
    h2 = (1, h_rel, h_in, goal_dev, goal_self)
    h3 = (2, dh_out, dh_rel, from_dev, from_self)
    h4 = (3, dh_rel, dh_in, src_dev, relays_self)
    w3 = (4, hw_out, hw_rel, from_dev, from_self)
    w4 = (5, hw_rel, hw_in, src_dev, relays_self)

    await_rows(p_from_xr, p_all, slot_of(xr, y))
    n_xr_yl = push(p_all, slot_of(xr, y), to_yl, A, HALF)
    push(p_all, slot_of(xr, y), to_yr, A, HALF, LAST)
    await_rows(p_from_yr, p_all, slot_of(x, yr))
    m_yr_xl = push(p_all, slot_of(x, yr), to_xl, B, HALF)
    push(p_all, slot_of(x, yr), to_xr, B, HALF, LAST)
    await_rows(p_from_xl, p_all, slot_of(xl, y))
    n_xl_yl = push(p_all, slot_of(xl, y), to_yl, A, HALF)
    push(p_all, slot_of(xl, y), to_yr, A, HALF, LAST)
    await_rows(p_from_yl, p_all, slot_of(x, yl))
    m_yl_xl = push(p_all, slot_of(x, yl), to_xl, B, HALF)
    push(p_all, slot_of(x, yl), to_xr, B, HALF, LAST)
    q4, q3l, q3s = [], [], []
    for hf in range(2):
        f = hf * HALF
        await_rows(q2[hf][0], q_all, qz(z - 2 * d, core), f, HALF)
        share(-2, f, HALF)
        q4.append(push(q_all, qz(z - 2 * d, core), z_dev(2 * d), f, HALF))
        q3l.append(push(q_all, qz(z - 2 * d, core), z_dev(d), f, HALF))
        await_rows(q2[hf][1], q_all, qz(z + 2 * d, core), f, HALF)
        share(2, f, HALF)
        q3s.append(push(q_all, qz(z + 2 * d, core), z_dev(-d), f, HALF))
    hop_start(*h1)
    await_rows(q1l, q_all, qz(z - d, core))
    share(-1)
    await_rows(q1s, q_all, qz(z + d, core))
    share(1)
    await_rows(p_from_x2, p_all, slot_of(x2, y))
    push(p_all, slot_of(x2, y), to_y2, A, HALF, LAST)
    push(p_all, slot_of(x2, y), to_yl, A, HALF, LAST)
    push(p_all, slot_of(x2, y), to_yr, A, HALF, LAST)
    await_rows(p_from_y2, p_all, slot_of(x, y2))
    push(p_all, slot_of(x, y2), to_x2, B, HALF, LAST)
    push(p_all, slot_of(x, y2), to_xl, B, HALF, LAST)
    push(p_all, slot_of(x, y2), to_xr, B, HALF, LAST)
    await_rows(n_xr_yl, p_all, slot_of(xr, yr), A, HALF)
    push(p_all, slot_of(xr, yr), to_yl, A, HALF, LAST)
    await_rows(m_yr_xl, p_all, slot_of(xr, yr), B, HALF)
    push(p_all, slot_of(xr, yr), to_xl, B, HALF, LAST)
    await_rows(n_xl_yl, p_all, slot_of(xl, yr), A, HALF)
    push(p_all, slot_of(xl, yr), to_yl, A, HALF, LAST)
    await_rows(m_yl_xl, p_all, slot_of(xr, yl), B, HALF)
    push(p_all, slot_of(xr, yl), to_xl, B, HALF, LAST)
    for hf in range(2):
        f = hf * HALF
        await_rows(q3s[hf], q_all, qz(z + 3 * d, core), f, HALF)
        share(3, f, HALF)
        await_rows(q3l[hf], q_all, qz(z - 3 * d, core), f, HALF)
        share(-3, f, HALF)
    for hf in range(2):
        f = hf * HALF
        await_rows(q4[hf], q_all, qz(z + 4, core), f, HALF)
        share(4, f, HALF)
    hop_recv(*h1)
    hop_start(*h2)

    arrive(LAST, p_all.at[pl.ds(0, 14 * HALF)])

    csum[...] = jnp.zeros_like(csum)

    def score(t, carry):
        first = pl.multiple_of(t * TILE, TILE)
        s = nt(q_all[pl.ds(first, TILE), :], p_all[...])
        e = jnp.exp(inverse_temp * s - inverse_temp)
        e_s[pl.ds(first, TILE), :] = e
        csum[...] += jnp.sum(e.reshape(TILE // 8, 8, GROUP), axis=0)
        part = e[:, :128]
        for j in range(1, GROUP // 128):
            part = part + e[:, j * 128 : (j + 1) * 128]
        for j in range(TILE // 128):
            row = jnp.sum(jnp.transpose(part[j * 128 : (j + 1) * 128, :]), axis=0, keepdims=True)
            tq[q_slot, pl.ds(t * (TILE // 128) + j, 1), :] = row
        return carry

    for i in range(2):
        score(core * 2 + i, 0)
    arrive(SHARED, q_all.at[pl.ds(0, 8 * ROWS)])
    for i in range(2):
        score((1 - core) * 2 + i, 0)
    total = jnp.sum(csum[...], axis=0, keepdims=True)
    for j in range(GROUP // 128):
        tp[p_slot, pl.ds(j, 1), :] = total[:, j * 128 : (j + 1) * 128]

    hop_recv(*h2)

    def block_rows(j):
        return pl.ds(pl.multiple_of((j // 2) * 512 + core * 256 + (j % 2) * 128, 128), 128)

    q_half = jnp.concatenate([q_all[block_rows(j), :] for j in range(4)], axis=0)
    idx_copy.wait()
    hidx = idx_s[y_hi * 2 + core] - (from_hi * 16 + q_slot_of(from_z)) * 512 - from_pb * ROWS
    hidx = jnp.concatenate(
        [hidx[j : j + 1, c * ROWS : (c + 1) * ROWS] for c in range(2) for j in range(4)], axis=1
    )
    named = lax.broadcasted_iota(jnp.int32, (ROWS, 512), 0) == hidx
    e_hard = jnp.exp(inverse_temp * nt(h_in[...], q_half) - inverse_temp)
    e_hard = jnp.where(named, e_hard, 0.0)
    eh[...] = e_hard
    dh_out[...] = jnp.dot(named.astype(bf16), q_half, preferred_element_type=f32).astype(bf16)
    hard_sum = jnp.sum(e_hard, axis=0, keepdims=True)
    for j in range(4):
        tq[q_slot, pl.ds((j // 2) * 4 + core * 2 + j % 2, 1), :] += hard_sum[:, j * 128 : (j + 1) * 128]

    eye = lax.broadcasted_iota(jnp.int32, (128, 128), 0) == lax.broadcasted_iota(jnp.int32, (128, 128), 1)

    def total_copies(k, count):
        first_q, first_p = (q_slot, p_slot) if count == 1 else (0, 0)
        return [
            pltpu.make_async_remote_copy(
                src_ref=ref.at[pl.ds(first, count)], dst_ref=ref.at[pl.ds(first, count)],
                send_sem=t_sem.at[2 * i], recv_sem=t_sem.at[2 * i + 1], device_id=to, device_id_type=pl.DeviceIdType.MESH,
            )
            for i, (ref, first, to) in enumerate(
                ((tq, first_q, q_peer((q_slot + k) % 16)), (tp, first_p, p_peer((p_slot + k) % 16)))
            )
        ]

    for k in range(1, 16):
        for copy in total_copies(k, 1):
            copy.start()

    hop_start(*h3)

    is_keeper = z == mine % 8
    kb = mine // 8
    ka = core

    @pl.when(is_keeper)
    def _():
        for j in range(4):
            q_rows = q_all[block_rows(j), :]
            p_rows = p_all[pl.ds(pl.multiple_of(kb * 512 + j * 128, 128), 128), :]
            diag = jnp.where(eye, inverse_temp * nt(q_rows, p_rows), 0.0)
            dg[j : j + 1, :] = jnp.sum(diag, axis=0, keepdims=True)

    def diag_copy(k, dst, to, at):
        return pltpu.make_async_remote_copy(
            src_ref=dg, dst_ref=dst, send_sem=dg_send.at[k], recv_sem=dg_recv.at[at],
            device_id=to, device_id_type=pl.DeviceIdType.MESH,
        )

    def keep(act):
        @pl.when(is_keeper)
        def _():
            for k in range(8):
                sq, sp = (k // 4) * 8 + ka * 4 + k % 4, kb * 8 + k

                @pl.when(sq != q_slot)
                def _():
                    act(diag_copy(k, dgq, q_peer(sq), 0))

                @pl.when(sp != p_slot)
                def _():
                    act(diag_copy(8 + k, dgp, p_peer(sp), 1))

    keep(lambda copy: copy.start())
    dgq_self = jnp.logical_and(is_keeper, z // 4 == ka)
    dgp_self = jnp.logical_and(is_keeper, p_slot // 8 == kb)

    @pl.when(dgq_self)
    def _():
        dgq[...] = dg[...]

    @pl.when(dgp_self)
    def _():
        dgp[...] = dg[...]

    def turn(k, carry):
        first = pl.multiple_of(k * CHUNK, CHUNK)
        wt[:, pl.ds(first, CHUNK)] = jnp.transpose(w[pl.ds(first, CHUNK), :])
        return carry

    lax.fori_loop(0, MODEL // CHUNK, turn, 0)
    all_sent(0)
    for copy in total_copies(1, 15):
        copy.wait()
    sq = jnp.sum(tq[...], axis=0)
    sp = jnp.sum(tp[...], axis=0)
    rinv = inverse_temp / sq
    cinv = inverse_temp / sp
    rin_s[...] = rinv
    lrow_s[0:8, :] = sq
    lrow_s[8:16, :] = sp

    hard_weight = jnp.concatenate([rin_s[pl.ds((j // 2) * 4 + core * 2 + j % 2, 1), :] for j in range(4)], axis=1)
    weighted = eh[...] * hard_weight
    gh[...] = weighted.astype(bf16)
    hw_out[...] = jnp.broadcast_to(jnp.sum(weighted, axis=1, keepdims=True), (ROWS, 128))
    hop_start(*w3)
    for j in range(8):
        rcol[j * 128 : (j + 1) * 128, :] = jnp.transpose(jnp.broadcast_to(rinv[j : j + 1, :], (128, 128)))
        crow[:, j * 128 : (j + 1) * 128] = jnp.broadcast_to(cinv[j : j + 1, :], (8, 128))
    tile_s[...] = tn(gh[...], h_in[...])

    @pl.when(is_keeper)
    def _():
        for j in range(4):
            r = block_rows(j)
            c = pl.multiple_of(kb * 512 + j * 128, 128)
            factor = rcol[r, :] + crow[0:1, pl.ds(c, 128)]
            e_s[r, pl.ds(c, 128)] -= jnp.where(eye, 2.0 * inverse_temp / factor, 0.0)

    def question_tile(t):
        first = pl.multiple_of(t * TILE, TILE)
        factor = wide(rcol[pl.ds(first, TILE), :], GROUP // 128) + crow[0:1, :]
        weights = (e_s[pl.ds(first, TILE), :] * factor).astype(bf16)
        g_s[pl.ds(first, TILE), :] = weights
        value = jnp.dot(weights, p_all[...], preferred_element_type=f32)
        here = (t % 2 == core).astype(f32)
        value = value + here * tile_s[pl.ds(pl.multiple_of((t // 2) * TILE, TILE), TILE), :]
        for j in range(4):
            dq[t // 2, (t % 2) * 4 + j] = value[j * ROWS : (j + 1) * ROWS, :].astype(bf16)

    def four(ref, i):
        return ref.at[pl.ds(i * 4, 4)]

    phase[0] = 1
    n_pt = []
    for i in range(2):
        question_tile((1 - core) * 2 + i)
        n_pt.append(remote(four(dq.at[1 - core], i), four(prt, i), other))
    hop_recv(*h3)
    hop_start(*h4)
    for i in range(2):
        question_tile(core * 2 + i)

    def passage_tile(yy):
        first = pl.multiple_of(yy * TILE, TILE)
        value = tn(g_s[:, pl.ds(first, TILE)], q_all[...]).astype(bf16)
        for j in range(4):
            dpa[yy, j] = value[j * ROWS : j * ROWS + HALF, :]
            dpb[j, yy] = value[j * ROWS + HALF : (j + 1) * ROWS, :]

    def pair(ref, i):
        return ref.at[pl.ds(i * 2, 2)]

    def half(ref, hf):
        return ref.at[pl.ds(hf * HALF, HALF)]

    n_b1, n_b1s = [], []

    def send_b(yy):
        n_b1.append(remote(dpb.at[x2, yy], b1.at[0, yy], to_xr))
        n_b1s.append(remote(dpb.at[xl, yy], b1.at[1, yy], to_xl))

    passage_tile(y2)
    n_a1 = [remote(pair(dpa.at[y2], i), pair(a1.at[0], i), to_yr) for i in range(2)]
    send_b(y2)
    for i in range(2):
        arrive(n_pt[i], four(prt, i))
        prt[i * 4 : i * 4 + 4] = (
            prt[i * 4 : i * 4 + 4].astype(f32) + dq[core, i * 4 : i * 4 + 4].astype(f32)
        ).astype(bf16)
    r4, r3l, r3s = [], [], []
    for hf in range(2):
        r4.append(remote(half(prt.at[zmod(z + 4)], hf), half(zr.at[0], hf), z_dev(-2 * d)))
        r3l.append(remote(half(prt.at[zmod(z - 3 * d)], hf), half(zr.at[1], hf), z_dev(-d)))
        r3s.append(remote(half(prt.at[zmod(z + 3 * d)], hf), half(zr.at[2], hf), z_dev(d)))
    r1l = remote(prt.at[zmod(z - d)], zin.at[0], z_dev(-d))
    r1s = remote(prt.at[zmod(z + d)], zin.at[1], z_dev(d))
    passage_tile(yl)
    n_a1s = remote(dpa.at[yl], a1.at[1], to_yl)
    send_b(yl)
    passage_tile(yr)
    send_b(yr)
    passage_tile(y)
    send_b(y)

    n_a1l, n_b1l = [], []
    for i in range(2):
        two = slice(i * 2, i * 2 + 2)
        arrive(n_a1[i], pair(a1.at[0], i))
        a1[0, two] = (a1[0, two].astype(f32) + dpa[yr, two].astype(f32)).astype(bf16)
        n_a1l.append(remote(pair(a1.at[0], i), pair(a1.at[2], i), to_yr))

    r2l, r2s = [], []
    for hf in range(2):
        part = slice(hf * HALF, (hf + 1) * HALF)
        arrive(r3s[hf], half(zr.at[2], hf))
        zr[2, part, :] = (zr[2, part, :].astype(f32) + prt[zmod(z + 2 * d), part, :].astype(f32)).astype(bf16)
        r2s.append(remote(half(zr.at[2], hf), half(zin.at[3], hf), z_dev(2 * d)))
        arrive(r3l[hf], half(zr.at[1], hf))
        arrive(r4[hf], half(zr.at[0], hf))
        zr[1, part, :] = (
            zr[1, part, :].astype(f32) + zr[0, part, :].astype(f32) + prt[zmod(z - 2 * d), part, :].astype(f32)
        ).astype(bf16)
        r2l.append(remote(half(zr.at[1], hf), half(zin.at[2], hf), z_dev(-2 * d)))

    for i, yy in enumerate((y2, yl, yr, y)):
        arrive(n_b1[i], b1.at[0, yy])
        b1[0, yy] = (b1[0, yy].astype(f32) + dpb[xr, yy].astype(f32)).astype(bf16)
        n_b1l.append(remote(b1.at[0, yy], b1.at[2, yy], to_xr))

    hop_recv(*w3)
    hop_start(*w4)

    arrive(n_a1s, a1.at[1])
    for i in range(2):
        arrive(n_a1l[i], pair(a1.at[2], i))
    a1[1] = (a1[1].astype(f32) + a1[2].astype(f32) + dpa[y].astype(f32)).astype(bf16)
    n_a2 = [remote(a1.at[1, xx], a2.at[i], to) for i, (xx, to) in enumerate(((x2, to_x2), (xl, to_xl), (xr, to_xr)))]
    for i, yy in enumerate((y2, yl, yr, y)):
        arrive(n_b1s[i], b1.at[1, yy])
        arrive(n_b1l[i], b1.at[2, yy])
    b1[1] = (b1[1].astype(f32) + b1[2].astype(f32) + dpb[x].astype(f32)).astype(bf16)
    n_b2 = [remote(b1.at[1, yy], b2.at[i], to) for i, (yy, to) in enumerate(((y2, to_y2), (yl, to_yl), (yr, to_yr)))]

    def back(grad, i, first, count):
        part = slice(i * ROWS + first, i * ROWS + first + count)
        u = unit[part, :]
        along = jnp.sum(grad * u, axis=1, keepdims=True)
        ge[part, :] = ((grad - u * along) * wide(scale[part, :], WIDTH // 128)).astype(bf16)

    keeper_q = mine % 8
    group_p = y_hi * 8 + z

    @pl.when(jnp.logical_not(dgq_self))
    def _():
        diag_copy(0, dgq, (pb, y_hi * 16 + keeper_q * 2 + z // 4), 0).wait_recv()

    @pl.when(jnp.logical_not(dgp_self))
    def _():
        diag_copy(0, dgp, (group_p // 2, (group_p % 2) * 16 + zc), 1).wait_recv()

    def loss(total_row, diag, first):
        value = inverse_temp + jnp.log(total_row) - diag
        return jnp.where(first, value[:, :ROWS], value[:, ROWS:])

    loss_s[0, 0:1, 0:ROWS] = loss(lrow_s[pl.ds(core * 4 + z // 2, 1), :], dgq[pl.ds(core * 2 + (z % 4) // 2, 1), :], z % 2 == 0)
    loss_s[1, 0:1, 0:ROWS] = loss(lrow_s[pl.ds(8 + y * 2 + x // 2, 1), :], dgp[pl.ds(y_lo * 2 + x // 2, 1), :], x % 2 == 0)
    loss_copies = [pltpu.make_async_copy(loss_s.at[i], ref, o_sem.at[3, i]) for i, ref in enumerate((lq_ref, lp_ref))]
    for copy in loss_copies:
        copy.start()

    hop_recv(*h4)
    hop_recv(*w4)
    grad_h = (dh_in[...].astype(f32) * wide(hw_in[...], WIDTH // 128)).astype(bf16)
    back(grad_h.astype(f32), 2, 0, ROWS)

    arrive(r1l, zin.at[0])
    arrive(r1s, zin.at[1])
    for hf in range(2):
        arrive(r2s[hf], half(zin.at[3], hf))
        arrive(r2l[hf], half(zin.at[2], hf))
    back(jnp.sum(zin[...].astype(f32), axis=0) + prt[z].astype(f32), 0, 0, ROWS)
    for i in range(3):
        arrive(n_a2[i], a2.at[i])
    back(jnp.sum(a2[...].astype(f32), axis=0) + a1[1, x].astype(f32), 1, 0, HALF)
    for i in range(3):
        arrive(n_b2[i], b2.at[i])
    back(jnp.sum(b2[...].astype(f32), axis=0) + b1[1, y].astype(f32), 1, HALF, HALF)

    def out_copies(k):
        columns = pl.ds(pl.multiple_of(k * CHUNK, CHUNK), CHUNK)
        return [
            pltpu.make_async_copy(out_s.at[pl.ds(i * ROWS, ROWS), columns], ref.at[:, columns], o_sem.at[i, k])
            for i, ref in enumerate((oq_ref, op_ref, oh_ref))
        ]

    def unproject(k, carry):
        first = pl.multiple_of(k * CHUNK, CHUNK)
        out_s[:, pl.ds(first, CHUNK)] = jnp.dot(
            ge[...], wt[:, pl.ds(first, CHUNK)], preferred_element_type=f32
        ).astype(bf16)
        for copy in out_copies(k):
            copy.start()
        return carry

    for k in range(MODEL // CHUNK):
        unproject(k, 0)

    all_sent(1)
    for h in (h1, h2, h3, h4, w3, w4):
        hop_sent(*h)
    keep(lambda copy: copy.wait_send())
    for k in range(MODEL // CHUNK):
        for copy in out_copies(k):
            copy.wait()
    for copy in loss_copies:
        copy.wait()


def hand_on(gq, gp, gh, lq, lp, oq, op, oh, olq, olp, stage, lstage, lflat, in_sem, out_sem):
    arrivals = [pltpu.make_async_copy(src, stage.at[i], in_sem.at[i]) for i, src in enumerate((gq, gp, gh))]
    losses = [pltpu.make_async_copy(src, lstage.at[i], in_sem.at[3 + i]) for i, src in enumerate((lq, lp))]
    leaving = [pltpu.make_async_copy(stage.at[i], dst, out_sem.at[i]) for i, dst in enumerate((oq, op, oh))]
    leaving += [pltpu.make_async_copy(lflat.at[i], dst, out_sem.at[3 + i]) for i, dst in enumerate((olq, olp))]
    for copy in losses + arrivals:
        copy.start()
    for i, copy in enumerate(losses):
        copy.wait()
        lflat[i, :] = lstage[i, 0, 0:ROWS]
        leaving[3 + i].start()
    for i, copy in enumerate(arrivals):
        copy.wait()
        leaving[i].start()
    for copy in leaving:
        copy.wait()


COPIES = 130


def shards(questions, passages, hard_rows, hard_index, projection):
    vmem = pl.BlockSpec(memory_space=pltpu.VMEM)
    hbm = pl.BlockSpec(memory_space=pl.ANY)
    out = jax.ShapeDtypeStruct((ROWS, MODEL), bf16)
    loss = jax.ShapeDtypeStruct((8, 128), f32)
    flat = jax.ShapeDtypeStruct((ROWS,), f32)
    V, D = pltpu.VMEM, pltpu.SemaphoreType.DMA
    gq, gp, gh, lq, lp = pl.pallas_call(
        kernel,
        out_shape=(out, out, out, loss, loss),
        in_specs=[hbm] * 5,
        out_specs=(hbm,) * 5,
        scratch_shapes=[
            V((3 * ROWS, MODEL), bf16),
            V((MODEL, WIDTH), bf16),
            V((WIDTH, MODEL), bf16),
            V((3 * ROWS, WIDTH), f32),
            V((3 * ROWS, WIDTH), f32),
            V((3 * ROWS, 128), f32),
            V((GROUP, WIDTH), bf16),
            V((GROUP, WIDTH), bf16),
            V((ROWS, WIDTH), bf16),
            V((ROWS, WIDTH), bf16),
            V((ROWS, WIDTH), bf16),
            V((ROWS, WIDTH), bf16),
            V((ROWS, WIDTH), bf16),
            V((ROWS, WIDTH), bf16),
            V((ROWS, 128), f32),
            V((ROWS, 128), f32),
            V((ROWS, 128), f32),
            V((ROWS, 512), f32),
            V((ROWS, 512), bf16),
            V((GROUP, GROUP), f32),
            V((GROUP, GROUP), bf16),
            V((512, WIDTH), f32),
            V((8, GROUP), f32),
            V((16, 8, 128), f32),
            V((16, 8, 128), f32),
            V((GROUP, 128), f32),
            V((8, GROUP), f32),
            V((8, 128), f32),
            V((8, 128), f32),
            V((8, 128), f32),
            V((8, 128), f32),
            V((16, 128), f32),
            V((2, 8, ROWS, WIDTH), bf16),
            V((8, ROWS, WIDTH), bf16),
            V((3, ROWS, WIDTH), bf16),
            V((4, ROWS, WIDTH), bf16),
            V((4, 4, HALF, WIDTH), bf16),
            V((4, 4, HALF, WIDTH), bf16),
            V((3, 4, HALF, WIDTH), bf16),
            V((3, 4, HALF, WIDTH), bf16),
            V((3, HALF, WIDTH), bf16),
            V((3, HALF, WIDTH), bf16),
            V((3 * ROWS, WIDTH), bf16),
            V((3 * ROWS, MODEL), bf16),
            V((4, 4, 128), jnp.int32),
            V((2, 8, 128), f32),
            D((4,)), D((MODEL // CHUNK,)),
            D((2,)), D((COPIES,)),
            D((4,)),
            D((16,)), D((2,)), D((12,)), D((4, MODEL // CHUNK)),
        ],
        compiler_params=pltpu.CompilerParams(
            collective_id=0, has_side_effects=True, vmem_limit_bytes=56 * 1024 * 1024
        ),
        cost_estimate=pl.CostEstimate(flops=8 * 10**9, bytes_accessed=10**7, transcendentals=10**6),
    )(questions, passages, hard_rows, hard_index.reshape(4, 4, 128), projection)
    return pl.pallas_call(
        hand_on,
        out_shape=(out, out, out, flat, flat),
        in_specs=(hbm,) * 5,
        out_specs=(hbm,) * 5,
        scratch_shapes=[V((3, ROWS, MODEL), bf16), V((2, 8, 128), f32), V((2, ROWS), f32), D((5,)), D((5,))],
        compiler_params=pltpu.CompilerParams(vmem_limit_bytes=56 * 1024 * 1024),
        cost_estimate=pl.CostEstimate(flops=0, bytes_accessed=3 * 10**6, transcendentals=0),
    )(gq, gp, gh, lq, lp)


def solution(mesh):
    in_specs = (P(("pb", "pa"), None), P(("pa", "pb"), None), P(("pa", "pb"), None), P("pb"), P())
    out_specs = (
        P(("pb", "pa"), None),
        P(("pa", "pb"), None),
        P(("pa", "pb"), None),
        P(("pb", "pa")),
        P(("pa", "pb")),
    )
    return jax.shard_map(shards, mesh=mesh, in_specs=in_specs, out_specs=out_specs, check_vma=False)
```

```python
import math

import jax
import jax.numpy as jnp
from jax import lax
from jax.experimental import pallas as pl
from jax.experimental.pallas import tpu as pltpu
from jax.sharding import PartitionSpec as P

inverse_temp = 40.0
epsilon = 1e-06
f32 = jnp.float32
bf16 = jnp.bfloat16

NZ, NX, NY = 8, 4, 4
ROWS = 64
HALF = 32
GROUP = 1024
WIDTH = 768
MODEL = 4096
CHUNK = 1024
TILE = 256


def nt(a, b):
    return lax.dot_general(a, b, (((1,), (1,)), ((), ())), preferred_element_type=f32)


def tn(a, b):
    return lax.dot_general(a, b, (((0,), (0,)), ((), ())), preferred_element_type=f32)


def wide(column, times):
    return jnp.concatenate([column] * times, axis=1)


def kernel(
    xq_ref, xp_ref, xh_ref, idx_ref, w_ref,
    oq_ref, op_ref, oh_ref, lq_ref, lp_ref,
    xs, w, wt, acc, unit, scale, q_all, p_all, h_own, h_rel, h_in, dh_out, dh_rel, dh_in, hw_out, hw_rel, hw_in, eh, gh,
    e_s, g_s, tile_s, csum, tq, tp, rcol, crow, rin_s, dg, dgq, dgp, lrow_s,
    dq, prt, zr, zin, dpa, dpb, a1, b1, a2, b2, ge, out_s,
    idx_s, loss_s,
    in_sem, w_sem, send, recv, t_sem, dg_send, dg_recv, hop_sem, o_sem,
):
    pb, pa = lax.axis_index("pb"), lax.axis_index("pa")
    x, y_lo = pb // 2, pb % 2
    y_hi, z, core = pa // 16, (pa // 2) % 8, pa % 2
    y = y_hi * 2 + y_lo
    d = 1 - 2 * core

    def device(xx, yy, zz, cc):
        return (xx * 2 + yy % 2, (yy // 2) * 16 + zz * 2 + cc)

    def zmod(v):
        return (v + 16) % 8

    def mod4(v):
        return (v + 8) % 4

    q_slot = core * 8 + z
    p_slot = y * 4 + x
    zc = z * 2 + core

    def q_slot_of(zz):
        return zz * 2 + core

    def q_peer(s):
        return (pb, y_hi * 16 + (s % 8) * 2 + s // 8)

    def p_peer(s):
        return device(s % 4, s // 4, z, core)

    def slot_of(xx, yy):
        return yy * 4 + xx

    def rows(ref, slot, first=0, count=ROWS):
        return ref.at[pl.ds(pl.multiple_of(slot * ROWS + first, HALF), count)]

    counter = [0]
    phase = [0]
    sent_rows = [0, 0]

    def remote(src, dst, to, at=None):
        n = counter[0] if at is None else at
        if at is None:
            counter[0] += 1
        sent_rows[phase[0]] += math.prod(src.shape) // WIDTH
        pltpu.make_async_remote_copy(
            src_ref=src, dst_ref=dst, send_sem=send.at[phase[0]], recv_sem=recv.at[n],
            device_id=to, device_id_type=pl.DeviceIdType.MESH,
        ).start()
        return n

    def arrive(n, dst):
        pltpu.make_async_remote_copy(
            src_ref=dst, dst_ref=dst, send_sem=send.at[0], recv_sem=recv.at[n],
            device_id=(pb, pa), device_id_type=pl.DeviceIdType.MESH,
        ).wait_recv()

    def all_sent(i):
        part = w.at[pl.ds(0, sent_rows[i])]
        pltpu.make_async_remote_copy(
            src_ref=part, dst_ref=part, send_sem=send.at[i], recv_sem=recv.at[0],
            device_id=(pb, pa), device_id_type=pl.DeviceIdType.MESH,
        ).wait_send()

    inputs = []
    idx_copy = pltpu.make_async_copy(idx_ref, idx_s, in_sem.at[3])
    for i, ref in enumerate((xq_ref, xp_ref, xh_ref)):
        copy = pltpu.make_async_copy(ref, xs.at[pl.ds(i * ROWS, ROWS)], in_sem.at[i])
        copy.start()
        inputs.append(copy)
    for k in range(MODEL // CHUNK):
        pltpu.make_async_copy(w_ref.at[pl.ds(k * CHUNK, CHUNK)], w.at[pl.ds(k * CHUNK, CHUNK)], w_sem.at[k]).start()

    idx_copy.start()

    barrier = pltpu.get_barrier_semaphore()

    def greet(k, carry):
        pl.semaphore_signal(barrier, inc=1, device_id=q_peer((q_slot + k) % 16), device_id_type=pl.DeviceIdType.MESH)
        pl.semaphore_signal(barrier, inc=1, device_id=p_peer((p_slot + k) % 16), device_id_type=pl.DeviceIdType.MESH)
        return carry

    lax.fori_loop(1, 16, greet, 0)

    for copy in inputs:
        copy.wait()
    acc[...] = jnp.zeros_like(acc)

    def project(k, carry):
        first = pl.multiple_of(k * CHUNK, CHUNK)
        pltpu.make_async_copy(w_ref.at[pl.ds(first, CHUNK)], w.at[pl.ds(first, CHUNK)], w_sem.at[k]).wait()
        acc[...] += jnp.dot(xs[:, pl.ds(first, CHUNK)], w[pl.ds(first, CHUNK), :], preferred_element_type=f32)
        return carry

    for k in range(MODEL // CHUNK):
        project(k, 0)

    def normalise(i):
        emb = acc[i * ROWS : (i + 1) * ROWS, :]
        s = lax.rsqrt(jnp.sum(emb * emb, axis=1, keepdims=True) + epsilon)
        u = emb * s
        scale[i * ROWS : (i + 1) * ROWS, :] = jnp.broadcast_to(s, (ROWS, 128))
        unit[i * ROWS : (i + 1) * ROWS, :] = u
        return u.astype(bf16)

    q_all[pl.ds(pl.multiple_of(q_slot * ROWS, ROWS), ROWS), :] = normalise(0)
    p_all[pl.ds(pl.multiple_of(p_slot * ROWS, ROWS), ROWS), :] = normalise(1)
    h_own[...] = normalise(2)
    pl.semaphore_wait(barrier, 30)

    def z_dev(v):
        return device(x, y, zmod(z + v), core)

    other = device(x, y, z, 1 - core)
    xl, xr, yl, yr = mod4(x + d), mod4(x - d), mod4(y + d), mod4(y - d)
    x2, y2 = mod4(x + 2), mod4(y + 2)
    to_xl, to_xr, to_x2 = device(xl, y, z, core), device(xr, y, z, core), device(x2, y, z, core)
    to_yl, to_yr, to_y2 = device(x, yl, z, core), device(x, yr, z, core), device(x, y2, z, core)

    def qz(zz, cc):
        return cc * 8 + zmod(zz)

    def push(ref, slot, to, first=0, count=ROWS, at=None):
        part = rows(ref, slot, first, count)
        return remote(part, part, to, at)

    def await_rows(n, ref, slot, first=0, count=ROWS):
        arrive(n, rows(ref, slot, first, count))

    SHARED, LAST = COPIES - 1, COPIES - 2

    def share(v, first=0, count=ROWS):
        push(q_all, qz(z + v * d, core), other, first, count, SHARED)

    A, B = 0, HALF
    share(0)
    q2 = [[push(q_all, q_slot, z_dev(2 * d), hf * HALF, HALF), push(q_all, q_slot, z_dev(-2 * d), hf * HALF, HALF)] for hf in range(2)]
    p_from_xr = push(p_all, p_slot, to_xl)
    p_from_xl = push(p_all, p_slot, to_xr)
    p_from_yr = push(p_all, p_slot, to_yl)
    p_from_yl = push(p_all, p_slot, to_yr)
    p_from_x2 = push(p_all, p_slot, to_x2)
    p_from_y2 = push(p_all, p_slot, to_y2)
    q1l = push(q_all, q_slot, z_dev(d))
    q1s = push(q_all, q_slot, z_dev(-d))

    def column(m):
        return m // 2, m % 2

    relay_dev = (pb, y_hi * 16 + zmod(z + d * pb) * 2 + core)
    src_z = zmod(z - d * pb)
    src_dev = (pb, y_hi * 16 + src_z * 2 + core)
    goal_pb, goal_hi = column(y_hi * 8 + src_z)
    goal_dev = (goal_pb, goal_hi * 16 + zc)
    mine = 2 * pb + y_hi
    from_hi, from_z = mine // 8, mine % 8
    from_pb = zmod(d * (z - from_z))
    from_dev = (from_pb, from_hi * 16 + zc)
    relays_self = pb == 0
    goal_self = jnp.logical_and(goal_pb == pb, goal_hi == y_hi)
    from_self = jnp.logical_and(from_pb == pb, from_hi == y_hi)

    def hop(k, src, dst, to):
        return pltpu.make_async_remote_copy(
            src_ref=src, dst_ref=dst, send_sem=hop_sem.at[2 * k], recv_sem=hop_sem.at[2 * k + 1],
            device_id=to, device_id_type=pl.DeviceIdType.MESH,
        )

    def hop_start(k, src, dst, to, is_self):
        @pl.when(jnp.logical_not(is_self))
        def _():
            hop(k, src, dst, to).start()

        @pl.when(is_self)
        def _():
            dst[...] = src[...]

    def hop_recv(k, src, dst, to, is_self):
        @pl.when(jnp.logical_not(is_self))
        def _():
            hop(k, src, dst, to).wait_recv()

    def hop_sent(k, src, dst, to, is_self):
        @pl.when(jnp.logical_not(is_self))
        def _():
            hop(k, src, dst, to).wait_send()

    h1 = (0, h_own, h_rel, relay_dev, relays_self)
    h2 = (1, h_rel, h_in, goal_dev, goal_self)
    h3 = (2, dh_out, dh_rel, from_dev, from_self)
    h4 = (3, dh_rel, dh_in, src_dev, relays_self)
    w3 = (4, hw_out, hw_rel, from_dev, from_self)
    w4 = (5, hw_rel, hw_in, src_dev, relays_self)

    hop_start(*h1)

    await_rows(p_from_xr, p_all, slot_of(xr, y))
    n_xr_yl = push(p_all, slot_of(xr, y), to_yl, A, HALF)
    push(p_all, slot_of(xr, y), to_yr, A, HALF, LAST)
    await_rows(p_from_yr, p_all, slot_of(x, yr))
    m_yr_xl = push(p_all, slot_of(x, yr), to_xl, B, HALF)
    push(p_all, slot_of(x, yr), to_xr, B, HALF, LAST)
    await_rows(p_from_xl, p_all, slot_of(xl, y))
    n_xl_yl = push(p_all, slot_of(xl, y), to_yl, A, HALF)
    push(p_all, slot_of(xl, y), to_yr, A, HALF, LAST)
    await_rows(p_from_yl, p_all, slot_of(x, yl))
    m_yl_xl = push(p_all, slot_of(x, yl), to_xl, B, HALF)
    push(p_all, slot_of(x, yl), to_xr, B, HALF, LAST)
    q4, q3l, q3s = [], [], []
    for hf in range(2):
        f = hf * HALF
        await_rows(q2[hf][0], q_all, qz(z - 2 * d, core), f, HALF)
        share(-2, f, HALF)
        q4.append(push(q_all, qz(z - 2 * d, core), z_dev(2 * d), f, HALF))
        q3l.append(push(q_all, qz(z - 2 * d, core), z_dev(d), f, HALF))
        await_rows(q2[hf][1], q_all, qz(z + 2 * d, core), f, HALF)
        share(2, f, HALF)
        q3s.append(push(q_all, qz(z + 2 * d, core), z_dev(-d), f, HALF))
    await_rows(q1l, q_all, qz(z - d, core))
    share(-1)
    await_rows(q1s, q_all, qz(z + d, core))
    share(1)
    await_rows(p_from_x2, p_all, slot_of(x2, y))
    push(p_all, slot_of(x2, y), to_y2, A, HALF, LAST)
    push(p_all, slot_of(x2, y), to_yl, A, HALF, LAST)
    push(p_all, slot_of(x2, y), to_yr, A, HALF, LAST)
    await_rows(p_from_y2, p_all, slot_of(x, y2))
    push(p_all, slot_of(x, y2), to_x2, B, HALF, LAST)
    push(p_all, slot_of(x, y2), to_xl, B, HALF, LAST)
    push(p_all, slot_of(x, y2), to_xr, B, HALF, LAST)
    await_rows(n_xr_yl, p_all, slot_of(xr, yr), A, HALF)
    push(p_all, slot_of(xr, yr), to_yl, A, HALF, LAST)
    await_rows(m_yr_xl, p_all, slot_of(xr, yr), B, HALF)
    push(p_all, slot_of(xr, yr), to_xl, B, HALF, LAST)
    await_rows(n_xl_yl, p_all, slot_of(xl, yr), A, HALF)
    push(p_all, slot_of(xl, yr), to_yl, A, HALF, LAST)
    await_rows(m_yl_xl, p_all, slot_of(xr, yl), B, HALF)
    push(p_all, slot_of(xr, yl), to_xl, B, HALF, LAST)
    hop_recv(*h1)
    hop_start(*h2)
    for hf in range(2):
        f = hf * HALF
        await_rows(q3s[hf], q_all, qz(z + 3 * d, core), f, HALF)
        share(3, f, HALF)
        await_rows(q3l[hf], q_all, qz(z - 3 * d, core), f, HALF)
        share(-3, f, HALF)
    for hf in range(2):
        f = hf * HALF
        await_rows(q4[hf], q_all, qz(z + 4, core), f, HALF)
        share(4, f, HALF)

    arrive(LAST, p_all.at[pl.ds(0, 14 * HALF)])

    csum[...] = jnp.zeros_like(csum)

    def score(t, carry):
        first = pl.multiple_of(t * TILE, TILE)
        s = nt(q_all[pl.ds(first, TILE), :], p_all[...])
        e = jnp.exp(inverse_temp * s - inverse_temp)
        e_s[pl.ds(first, TILE), :] = e
        csum[...] += jnp.sum(e.reshape(TILE // 8, 8, GROUP), axis=0)
        part = e[:, :128]
        for j in range(1, GROUP // 128):
            part = part + e[:, j * 128 : (j + 1) * 128]
        for j in range(TILE // 128):
            row = jnp.sum(jnp.transpose(part[j * 128 : (j + 1) * 128, :]), axis=0, keepdims=True)
            tq[q_slot, pl.ds(t * (TILE // 128) + j, 1), :] = row
        return carry

    for i in range(2):
        score(core * 2 + i, 0)
    arrive(SHARED, q_all.at[pl.ds(0, 8 * ROWS)])
    for i in range(2):
        score((1 - core) * 2 + i, 0)
    total = jnp.sum(csum[...], axis=0, keepdims=True)
    for j in range(GROUP // 128):
        tp[p_slot, pl.ds(j, 1), :] = total[:, j * 128 : (j + 1) * 128]

    def total_copies(k, count):
        first_q, first_p = (q_slot, p_slot) if count == 1 else (0, 0)
        return [
            pltpu.make_async_remote_copy(
                src_ref=ref.at[pl.ds(first, count)], dst_ref=ref.at[pl.ds(first, count)],
                send_sem=t_sem.at[2 * i], recv_sem=t_sem.at[2 * i + 1], device_id=to, device_id_type=pl.DeviceIdType.MESH,
            )
            for i, (ref, first, to) in enumerate(
                ((tq, first_q, q_peer((q_slot + k) % 16)), (tp, first_p, p_peer((p_slot + k) % 16)))
            )
        ]

    for k in (10, 9, 11, 6, 14, 2, 8, 5, 7, 13, 15, 1, 3, 4, 12):
        total_copies(k, 1)[1].start()

    hop_recv(*h2)

    def block_rows(j):
        return pl.ds(pl.multiple_of((j // 2) * 512 + core * 256 + (j % 2) * 128, 128), 128)

    q_half = jnp.concatenate([q_all[block_rows(j), :] for j in range(4)], axis=0)
    idx_copy.wait()
    hidx = idx_s[y_hi * 2 + core] - (from_hi * 16 + q_slot_of(from_z)) * 512 - from_pb * ROWS
    hidx = jnp.concatenate(
        [hidx[j : j + 1, c * ROWS : (c + 1) * ROWS] for c in range(2) for j in range(4)], axis=1
    )
    named = lax.broadcasted_iota(jnp.int32, (ROWS, 512), 0) == hidx
    e_hard = jnp.exp(inverse_temp * nt(h_in[...], q_half) - inverse_temp)
    e_hard = jnp.where(named, e_hard, 0.0)
    eh[...] = e_hard
    hard_sum = jnp.sum(e_hard, axis=0, keepdims=True)
    for j in range(4):
        tq[q_slot, pl.ds((j // 2) * 4 + core * 2 + j % 2, 1), :] += hard_sum[:, j * 128 : (j + 1) * 128]

    eye = lax.broadcasted_iota(jnp.int32, (128, 128), 0) == lax.broadcasted_iota(jnp.int32, (128, 128), 1)

    for k in (4, 12, 5, 3, 11, 13, 6, 2, 10, 14, 7, 1, 9, 15, 8):
        total_copies(k, 1)[0].start()

    dh_out[...] = jnp.dot(named.astype(bf16), q_half, preferred_element_type=f32).astype(bf16)
    hop_start(*h3)

    is_keeper = z == mine % 8
    kb = mine // 8
    ka = core

    @pl.when(is_keeper)
    def _():
        for j in range(4):
            q_rows = q_all[block_rows(j), :]
            p_rows = p_all[pl.ds(pl.multiple_of(kb * 512 + j * 128, 128), 128), :]
            diag = jnp.where(eye, inverse_temp * nt(q_rows, p_rows), 0.0)
            dg[j : j + 1, :] = jnp.sum(diag, axis=0, keepdims=True)

    def diag_copy(k, dst, to, at):
        return pltpu.make_async_remote_copy(
            src_ref=dg, dst_ref=dst, send_sem=dg_send.at[k], recv_sem=dg_recv.at[at],
            device_id=to, device_id_type=pl.DeviceIdType.MESH,
        )

    def keep(act):
        @pl.when(is_keeper)
        def _():
            for k in range(8):
                sq, sp = (k // 4) * 8 + ka * 4 + k % 4, kb * 8 + k

                @pl.when(sq != q_slot)
                def _():
                    act(diag_copy(k, dgq, q_peer(sq), 0))

                @pl.when(sp != p_slot)
                def _():
                    act(diag_copy(8 + k, dgp, p_peer(sp), 1))

    keep(lambda copy: copy.start())
    dgq_self = jnp.logical_and(is_keeper, z // 4 == ka)
    dgp_self = jnp.logical_and(is_keeper, p_slot // 8 == kb)

    @pl.when(dgq_self)
    def _():
        dgq[...] = dg[...]

    @pl.when(dgp_self)
    def _():
        dgp[...] = dg[...]

    def turn(k, carry):
        first = pl.multiple_of(k * CHUNK, CHUNK)
        wt[:, pl.ds(first, CHUNK)] = jnp.transpose(w[pl.ds(first, CHUNK), :])
        return carry

    lax.fori_loop(0, MODEL // CHUNK, turn, 0)
    all_sent(0)
    for copy in total_copies(1, 15):
        copy.wait()
    sq = jnp.sum(tq[...], axis=0)
    sp = jnp.sum(tp[...], axis=0)
    rinv = inverse_temp / sq
    cinv = inverse_temp / sp
    rin_s[...] = rinv
    lrow_s[0:8, :] = sq
    lrow_s[8:16, :] = sp

    hard_weight = jnp.concatenate([rin_s[pl.ds((j // 2) * 4 + core * 2 + j % 2, 1), :] for j in range(4)], axis=1)
    weighted = eh[...] * hard_weight
    gh[...] = weighted.astype(bf16)
    hw_out[...] = jnp.broadcast_to(jnp.sum(weighted, axis=1, keepdims=True), (ROWS, 128))
    hop_start(*w3)
    for j in range(8):
        rcol[j * 128 : (j + 1) * 128, :] = jnp.transpose(jnp.broadcast_to(rinv[j : j + 1, :], (128, 128)))
        crow[:, j * 128 : (j + 1) * 128] = jnp.broadcast_to(cinv[j : j + 1, :], (8, 128))
    tile_s[...] = tn(gh[...], h_in[...])

    @pl.when(is_keeper)
    def _():
        for j in range(4):
            r = block_rows(j)
            c = pl.multiple_of(kb * 512 + j * 128, 128)
            factor = rcol[r, :] + crow[0:1, pl.ds(c, 128)]
            e_s[r, pl.ds(c, 128)] -= jnp.where(eye, 2.0 * inverse_temp / factor, 0.0)

    def question_tile(t):
        first = pl.multiple_of(t * TILE, TILE)
        factor = wide(rcol[pl.ds(first, TILE), :], GROUP // 128) + crow[0:1, :]
        weights = (e_s[pl.ds(first, TILE), :] * factor).astype(bf16)
        g_s[pl.ds(first, TILE), :] = weights
        value = jnp.dot(weights, p_all[...], preferred_element_type=f32)
        here = (t % 2 == core).astype(f32)
        value = value + here * tile_s[pl.ds(pl.multiple_of((t // 2) * TILE, TILE), TILE), :]
        for j in range(4):
            dq[t // 2, (t % 2) * 4 + j] = value[j * ROWS : (j + 1) * ROWS, :].astype(bf16)

    def four(ref, i):
        return ref.at[pl.ds(i * 4, 4)]

    phase[0] = 1
    n_pt = []
    for i in range(2):
        question_tile((1 - core) * 2 + i)
        n_pt.append(remote(four(dq.at[1 - core], i), four(prt, i), other))
    hop_recv(*h3)
    hop_start(*h4)
    for i in range(2):
        question_tile(core * 2 + i)

    def passage_tile(yy):
        first = pl.multiple_of(yy * TILE, TILE)
        value = tn(g_s[:, pl.ds(first, TILE)], q_all[...]).astype(bf16)
        for j in range(4):
            dpa[yy, j] = value[j * ROWS : j * ROWS + HALF, :]
            dpb[j, yy] = value[j * ROWS + HALF : (j + 1) * ROWS, :]

    def pair(ref, i):
        return ref.at[pl.ds(i * 2, 2)]

    def half(ref, hf):
        return ref.at[pl.ds(hf * HALF, HALF)]

    n_b1, n_b1s = [], []

    def send_b(yy):
        n_b1.append(remote(dpb.at[x2, yy], b1.at[0, yy], to_xr))
        n_b1s.append(remote(dpb.at[xl, yy], b1.at[1, yy], to_xl))

    passage_tile(y2)
    n_a1 = [remote(pair(dpa.at[y2], i), pair(a1.at[0], i), to_yr) for i in range(2)]
    send_b(y2)
    for i in range(2):
        arrive(n_pt[i], four(prt, i))
        prt[i * 4 : i * 4 + 4] = (
            prt[i * 4 : i * 4 + 4].astype(f32) + dq[core, i * 4 : i * 4 + 4].astype(f32)
        ).astype(bf16)
    r4, r3l, r3s = [], [], []
    for hf in range(2):
        r4.append(remote(half(prt.at[zmod(z + 4)], hf), half(zr.at[0], hf), z_dev(-2 * d)))
        r3l.append(remote(half(prt.at[zmod(z - 3 * d)], hf), half(zr.at[1], hf), z_dev(-d)))
        r3s.append(remote(half(prt.at[zmod(z + 3 * d)], hf), half(zr.at[2], hf), z_dev(d)))
    r1l = remote(prt.at[zmod(z - d)], zin.at[0], z_dev(-d))
    r1s = remote(prt.at[zmod(z + d)], zin.at[1], z_dev(d))
    passage_tile(yl)
    n_a1s = remote(dpa.at[yl], a1.at[1], to_yl)
    send_b(yl)
    passage_tile(yr)
    send_b(yr)
    passage_tile(y)
    send_b(y)

    n_a1l, n_b1l = [], []
    for i in range(2):
        two = slice(i * 2, i * 2 + 2)
        arrive(n_a1[i], pair(a1.at[0], i))
        a1[0, two] = (a1[0, two].astype(f32) + dpa[yr, two].astype(f32)).astype(bf16)
        n_a1l.append(remote(pair(a1.at[0], i), pair(a1.at[2], i), to_yr))

    r2l, r2s = [], []
    def q_relay(hf):
        part = slice(hf * HALF, (hf + 1) * HALF)
        arrive(r3s[hf], half(zr.at[2], hf))
        zr[2, part, :] = (zr[2, part, :].astype(f32) + prt[zmod(z + 2 * d), part, :].astype(f32)).astype(bf16)
        r2s.append(remote(half(zr.at[2], hf), half(zin.at[3], hf), z_dev(2 * d)))
        arrive(r3l[hf], half(zr.at[1], hf))
        arrive(r4[hf], half(zr.at[0], hf))
        zr[1, part, :] = (
            zr[1, part, :].astype(f32) + zr[0, part, :].astype(f32) + prt[zmod(z - 2 * d), part, :].astype(f32)
        ).astype(bf16)
        r2l.append(remote(half(zr.at[1], hf), half(zin.at[2], hf), z_dev(-2 * d)))

    def b_relay(i, yy):
        arrive(n_b1[i], b1.at[0, yy])
        b1[0, yy] = (b1[0, yy].astype(f32) + dpb[xr, yy].astype(f32)).astype(bf16)
        n_b1l.append(remote(b1.at[0, yy], b1.at[2, yy], to_xr))

    b_relay(0, y2)
    b_relay(1, yl)
    q_relay(0)
    b_relay(2, yr)
    b_relay(3, y)
    q_relay(1)

    hop_recv(*w3)
    hop_start(*w4)

    arrive(n_a1s, a1.at[1])
    for i in range(2):
        arrive(n_a1l[i], pair(a1.at[2], i))
    a1[1] = (a1[1].astype(f32) + a1[2].astype(f32) + dpa[y].astype(f32)).astype(bf16)
    n_a2 = [remote(a1.at[1, xx], a2.at[i], to) for i, (xx, to) in enumerate(((x2, to_x2), (xl, to_xl), (xr, to_xr)))]
    for i, yy in enumerate((y2, yl, yr, y)):
        arrive(n_b1s[i], b1.at[1, yy])
        arrive(n_b1l[i], b1.at[2, yy])
    b1[1] = (b1[1].astype(f32) + b1[2].astype(f32) + dpb[x].astype(f32)).astype(bf16)
    n_b2 = [remote(b1.at[1, yy], b2.at[i], to) for i, (yy, to) in enumerate(((y2, to_y2), (yl, to_yl), (yr, to_yr)))]

    def back(grad, i, first, count):
        part = slice(i * ROWS + first, i * ROWS + first + count)
        u = unit[part, :]
        along = jnp.sum(grad * u, axis=1, keepdims=True)
        ge[part, :] = ((grad - u * along) * wide(scale[part, :], WIDTH // 128)).astype(bf16)

    keeper_q = mine % 8
    group_p = y_hi * 8 + z

    @pl.when(jnp.logical_not(dgq_self))
    def _():
        diag_copy(0, dgq, (pb, y_hi * 16 + keeper_q * 2 + z // 4), 0).wait_recv()

    @pl.when(jnp.logical_not(dgp_self))
    def _():
        diag_copy(0, dgp, (group_p // 2, (group_p % 2) * 16 + zc), 1).wait_recv()

    def loss(total_row, diag, first):
        value = inverse_temp + jnp.log(total_row) - diag
        return jnp.where(first, value[:, :ROWS], value[:, ROWS:])

    loss_s[0, 0:1, 0:ROWS] = loss(lrow_s[pl.ds(core * 4 + z // 2, 1), :], dgq[pl.ds(core * 2 + (z % 4) // 2, 1), :], z % 2 == 0)
    loss_s[1, 0:1, 0:ROWS] = loss(lrow_s[pl.ds(8 + y * 2 + x // 2, 1), :], dgp[pl.ds(y_lo * 2 + x // 2, 1), :], x % 2 == 0)
    loss_copies = [pltpu.make_async_copy(loss_s.at[i], ref, o_sem.at[3, i]) for i, ref in enumerate((lq_ref, lp_ref))]
    for copy in loss_copies:
        copy.start()

    hop_recv(*h4)
    hop_recv(*w4)
    grad_h = (dh_in[...].astype(f32) * wide(hw_in[...], WIDTH // 128)).astype(bf16)
    back(grad_h.astype(f32), 2, 0, ROWS)

    arrive(r1l, zin.at[0])
    arrive(r1s, zin.at[1])
    for hf in range(2):
        arrive(r2s[hf], half(zin.at[3], hf))
        arrive(r2l[hf], half(zin.at[2], hf))
    back(jnp.sum(zin[...].astype(f32), axis=0) + prt[z].astype(f32), 0, 0, ROWS)
    for i in range(3):
        arrive(n_a2[i], a2.at[i])
    back(jnp.sum(a2[...].astype(f32), axis=0) + a1[1, x].astype(f32), 1, 0, HALF)
    for i in range(3):
        arrive(n_b2[i], b2.at[i])
    back(jnp.sum(b2[...].astype(f32), axis=0) + b1[1, y].astype(f32), 1, HALF, HALF)

    def out_copies(k):
        columns = pl.ds(pl.multiple_of(k * CHUNK, CHUNK), CHUNK)
        return [
            pltpu.make_async_copy(out_s.at[pl.ds(i * ROWS, ROWS), columns], ref.at[:, columns], o_sem.at[i, k])
            for i, ref in enumerate((oq_ref, op_ref, oh_ref))
        ]

    def unproject(k, carry):
        first = pl.multiple_of(k * CHUNK, CHUNK)
        out_s[:, pl.ds(first, CHUNK)] = jnp.dot(
            ge[...], wt[:, pl.ds(first, CHUNK)], preferred_element_type=f32
        ).astype(bf16)
        for copy in out_copies(k):
            copy.start()
        return carry

    for k in range(MODEL // CHUNK):
        unproject(k, 0)

    all_sent(1)
    for h in (h1, h2, h3, h4, w3, w4):
        hop_sent(*h)
    keep(lambda copy: copy.wait_send())
    for k in range(MODEL // CHUNK):
        for copy in out_copies(k):
            copy.wait()
    for copy in loss_copies:
        copy.wait()


def hand_on(gq, gp, gh, lq, lp, oq, op, oh, olq, olp, stage, lstage, lflat, in_sem, out_sem):
    arrivals = [pltpu.make_async_copy(src, stage.at[i], in_sem.at[i]) for i, src in enumerate((gq, gp, gh))]
    losses = [pltpu.make_async_copy(src, lstage.at[i], in_sem.at[3 + i]) for i, src in enumerate((lq, lp))]
    leaving = [pltpu.make_async_copy(stage.at[i], dst, out_sem.at[i]) for i, dst in enumerate((oq, op, oh))]
    leaving += [pltpu.make_async_copy(lflat.at[i], dst, out_sem.at[3 + i]) for i, dst in enumerate((olq, olp))]
    for copy in losses + arrivals:
        copy.start()
    for i, copy in enumerate(losses):
        copy.wait()
        lflat[i, :] = lstage[i, 0, 0:ROWS]
        leaving[3 + i].start()
    for i, copy in enumerate(arrivals):
        copy.wait()
        leaving[i].start()
    for copy in leaving:
        copy.wait()


COPIES = 130


def shards(questions, passages, hard_rows, hard_index, projection):
    vmem = pl.BlockSpec(memory_space=pltpu.VMEM)
    hbm = pl.BlockSpec(memory_space=pl.ANY)
    out = jax.ShapeDtypeStruct((ROWS, MODEL), bf16)
    loss = jax.ShapeDtypeStruct((8, 128), f32)
    flat = jax.ShapeDtypeStruct((ROWS,), f32)
    V, D = pltpu.VMEM, pltpu.SemaphoreType.DMA
    gq, gp, gh, lq, lp = pl.pallas_call(
        kernel,
        out_shape=(out, out, out, loss, loss),
        in_specs=[hbm] * 5,
        out_specs=(hbm,) * 5,
        scratch_shapes=[
            V((3 * ROWS, MODEL), bf16),
            V((MODEL, WIDTH), bf16),
            V((WIDTH, MODEL), bf16),
            V((3 * ROWS, WIDTH), f32),
            V((3 * ROWS, WIDTH), f32),
            V((3 * ROWS, 128), f32),
            V((GROUP, WIDTH), bf16),
            V((GROUP, WIDTH), bf16),
            V((ROWS, WIDTH), bf16),
            V((ROWS, WIDTH), bf16),
            V((ROWS, WIDTH), bf16),
            V((ROWS, WIDTH), bf16),
            V((ROWS, WIDTH), bf16),
            V((ROWS, WIDTH), bf16),
            V((ROWS, 128), f32),
            V((ROWS, 128), f32),
            V((ROWS, 128), f32),
            V((ROWS, 512), f32),
            V((ROWS, 512), bf16),
            V((GROUP, GROUP), f32),
            V((GROUP, GROUP), bf16),
            V((512, WIDTH), f32),
            V((8, GROUP), f32),
            V((16, 8, 128), f32),
            V((16, 8, 128), f32),
            V((GROUP, 128), f32),
            V((8, GROUP), f32),
            V((8, 128), f32),
            V((8, 128), f32),
            V((8, 128), f32),
            V((8, 128), f32),
            V((16, 128), f32),
            V((2, 8, ROWS, WIDTH), bf16),
            V((8, ROWS, WIDTH), bf16),
            V((3, ROWS, WIDTH), bf16),
            V((4, ROWS, WIDTH), bf16),
            V((4, 4, HALF, WIDTH), bf16),
            V((4, 4, HALF, WIDTH), bf16),
            V((3, 4, HALF, WIDTH), bf16),
            V((3, 4, HALF, WIDTH), bf16),
            V((3, HALF, WIDTH), bf16),
            V((3, HALF, WIDTH), bf16),
            V((3 * ROWS, WIDTH), bf16),
            V((3 * ROWS, MODEL), bf16),
            V((4, 4, 128), jnp.int32),
            V((2, 8, 128), f32),
            D((4,)), D((MODEL // CHUNK,)),
            D((2,)), D((COPIES,)),
            D((4,)),
            D((16,)), D((2,)), D((12,)), D((4, MODEL // CHUNK)),
        ],
        compiler_params=pltpu.CompilerParams(
            collective_id=0, has_side_effects=True, vmem_limit_bytes=56 * 1024 * 1024
        ),
        cost_estimate=pl.CostEstimate(flops=8 * 10**9, bytes_accessed=10**7, transcendentals=10**6),
    )(questions, passages, hard_rows, hard_index.reshape(4, 4, 128), projection)
    return pl.pallas_call(
        hand_on,
        out_shape=(out, out, out, flat, flat),
        in_specs=(hbm,) * 5,
        out_specs=(hbm,) * 5,
        scratch_shapes=[V((3, ROWS, MODEL), bf16), V((2, 8, 128), f32), V((2, ROWS), f32), D((5,)), D((5,))],
        compiler_params=pltpu.CompilerParams(vmem_limit_bytes=56 * 1024 * 1024),
        cost_estimate=pl.CostEstimate(flops=0, bytes_accessed=3 * 10**6, transcendentals=0),
    )(gq, gp, gh, lq, lp)


def solution(mesh):
    in_specs = (P(("pb", "pa"), None), P(("pa", "pb"), None), P(("pa", "pb"), None), P("pb"), P())
    out_specs = (
        P(("pb", "pa"), None),
        P(("pa", "pb"), None),
        P(("pa", "pb"), None),
        P(("pb", "pa")),
        P(("pa", "pb")),
    )
    return jax.shard_map(shards, mesh=mesh, in_specs=in_specs, out_specs=out_specs, check_vma=False)
```

```python
import math

import jax
import jax.numpy as jnp
from jax import lax
from jax.experimental import pallas as pl
from jax.experimental.pallas import tpu as pltpu
from jax.sharding import PartitionSpec as P

inverse_temp = 40.0
epsilon = 1e-06
f32 = jnp.float32
bf16 = jnp.bfloat16

NZ, NX, NY = 8, 4, 4
ROWS = 64
HALF = 32
GROUP = 1024
WIDTH = 768
MODEL = 4096
CHUNK = 1024
TILE = 256


def nt(a, b):
    return lax.dot_general(a, b, (((1,), (1,)), ((), ())), preferred_element_type=f32)


def tn(a, b):
    return lax.dot_general(a, b, (((0,), (0,)), ((), ())), preferred_element_type=f32)


def wide(column, times):
    return jnp.concatenate([column] * times, axis=1)


def kernel(
    xq_ref, xp_ref, xh_ref, idx_ref, w_ref,
    oq_ref, op_ref, oh_ref, lq_ref, lp_ref,
    xs, w, wt, acc, unit, scale, q_all, p_all, h_own, h_rel, h_in, dh_out, dh_rel, dh_in, hw_out, hw_rel, hw_in, eh, gh,
    e_s, g_s, tile_s, csum, tq, tp, rcol, crow, rin_s, dg, dgq, dgp, lrow_s,
    dq, prt, zr, zin, dpa, dpb, a1, b1, a2, b2, ge, out_s,
    idx_s, loss_s,
    in_sem, w_sem, send, recv, t_sem, dg_send, dg_recv, hop_sem, o_sem,
):
    pb, pa = lax.axis_index("pb"), lax.axis_index("pa")
    x, y_lo = pb // 2, pb % 2
    y_hi, z, core = pa // 16, (pa // 2) % 8, pa % 2
    y = y_hi * 2 + y_lo
    d = 1 - 2 * core

    def device(xx, yy, zz, cc):
        return (xx * 2 + yy % 2, (yy // 2) * 16 + zz * 2 + cc)

    def zmod(v):
        return (v + 16) % 8

    def mod4(v):
        return (v + 8) % 4

    q_slot = core * 8 + z
    p_slot = y * 4 + x
    zc = z * 2 + core

    def q_slot_of(zz):
        return zz * 2 + core

    def q_peer(s):
        return (pb, y_hi * 16 + (s % 8) * 2 + s // 8)

    def p_peer(s):
        return device(s % 4, s // 4, z, core)

    def slot_of(xx, yy):
        return yy * 4 + xx

    def rows(ref, slot, first=0, count=ROWS):
        return ref.at[pl.ds(pl.multiple_of(slot * ROWS + first, HALF), count)]

    counter = [0]
    phase = [0]
    sent_rows = [0, 0]

    def remote(src, dst, to, at=None):
        n = counter[0] if at is None else at
        if at is None:
            counter[0] += 1
        sent_rows[phase[0]] += math.prod(src.shape) // WIDTH
        pltpu.make_async_remote_copy(
            src_ref=src, dst_ref=dst, send_sem=send.at[phase[0]], recv_sem=recv.at[n],
            device_id=to, device_id_type=pl.DeviceIdType.MESH,
        ).start()
        return n

    def arrive(n, dst):
        pltpu.make_async_remote_copy(
            src_ref=dst, dst_ref=dst, send_sem=send.at[0], recv_sem=recv.at[n],
            device_id=(pb, pa), device_id_type=pl.DeviceIdType.MESH,
        ).wait_recv()

    def all_sent(i):
        part = w.at[pl.ds(0, sent_rows[i])]
        pltpu.make_async_remote_copy(
            src_ref=part, dst_ref=part, send_sem=send.at[i], recv_sem=recv.at[0],
            device_id=(pb, pa), device_id_type=pl.DeviceIdType.MESH,
        ).wait_send()

    inputs = []
    idx_copy = pltpu.make_async_copy(idx_ref, idx_s, in_sem.at[3])
    for i, ref in enumerate((xq_ref, xp_ref, xh_ref)):
        copy = pltpu.make_async_copy(ref, xs.at[pl.ds(i * ROWS, ROWS)], in_sem.at[i])
        copy.start()
        inputs.append(copy)
    for k in range(MODEL // CHUNK):
        pltpu.make_async_copy(w_ref.at[pl.ds(k * CHUNK, CHUNK)], w.at[pl.ds(k * CHUNK, CHUNK)], w_sem.at[k]).start()

    idx_copy.start()

    barrier = pltpu.get_barrier_semaphore()

    def greet(k, carry):
        pl.semaphore_signal(barrier, inc=1, device_id=q_peer((q_slot + k) % 16), device_id_type=pl.DeviceIdType.MESH)
        pl.semaphore_signal(barrier, inc=1, device_id=p_peer((p_slot + k) % 16), device_id_type=pl.DeviceIdType.MESH)
        return carry

    lax.fori_loop(1, 16, greet, 0)

    for copy in inputs:
        copy.wait()
    acc[...] = jnp.zeros_like(acc)

    def project(k, carry):
        first = pl.multiple_of(k * CHUNK, CHUNK)
        pltpu.make_async_copy(w_ref.at[pl.ds(first, CHUNK)], w.at[pl.ds(first, CHUNK)], w_sem.at[k]).wait()
        acc[...] += jnp.dot(xs[:, pl.ds(first, CHUNK)], w[pl.ds(first, CHUNK), :], preferred_element_type=f32)
        return carry

    for k in range(MODEL // CHUNK):
        project(k, 0)

    def normalise(i):
        emb = acc[i * ROWS : (i + 1) * ROWS, :]
        s = lax.rsqrt(jnp.sum(emb * emb, axis=1, keepdims=True) + epsilon)
        u = emb * s
        scale[i * ROWS : (i + 1) * ROWS, :] = jnp.broadcast_to(s, (ROWS, 128))
        unit[i * ROWS : (i + 1) * ROWS, :] = u
        return u.astype(bf16)

    q_all[pl.ds(pl.multiple_of(q_slot * ROWS, ROWS), ROWS), :] = normalise(0)
    p_all[pl.ds(pl.multiple_of(p_slot * ROWS, ROWS), ROWS), :] = normalise(1)
    h_own[...] = normalise(2)
    pl.semaphore_wait(barrier, 30)

    def z_dev(v):
        return device(x, y, zmod(z + v), core)

    other = device(x, y, z, 1 - core)
    xl, xr, yl, yr = mod4(x + d), mod4(x - d), mod4(y + d), mod4(y - d)
    x2, y2 = mod4(x + 2), mod4(y + 2)
    to_xl, to_xr, to_x2 = device(xl, y, z, core), device(xr, y, z, core), device(x2, y, z, core)
    to_yl, to_yr, to_y2 = device(x, yl, z, core), device(x, yr, z, core), device(x, y2, z, core)

    def qz(zz, cc):
        return cc * 8 + zmod(zz)

    def push(ref, slot, to, first=0, count=ROWS, at=None):
        part = rows(ref, slot, first, count)
        return remote(part, part, to, at)

    def await_rows(n, ref, slot, first=0, count=ROWS):
        arrive(n, rows(ref, slot, first, count))

    SHARED, LAST = COPIES - 1, COPIES - 2

    def share(v, first=0, count=ROWS):
        push(q_all, qz(z + v * d, core), other, first, count, SHARED)

    A, B = 0, HALF
    share(0)
    q2 = [[push(q_all, q_slot, z_dev(2 * d), hf * HALF, HALF), push(q_all, q_slot, z_dev(-2 * d), hf * HALF, HALF)] for hf in range(2)]
    p_from_xr = push(p_all, p_slot, to_xl)
    p_from_xl = push(p_all, p_slot, to_xr)
    p_from_yr = push(p_all, p_slot, to_yl)
    p_from_yl = push(p_all, p_slot, to_yr)
    p_from_x2 = push(p_all, p_slot, to_x2)
    p_from_y2 = push(p_all, p_slot, to_y2)
    q1l = push(q_all, q_slot, z_dev(d))
    q1s = push(q_all, q_slot, z_dev(-d))

    def column(m):
        return m // 2, m % 2

    relay_dev = (pb, y_hi * 16 + zmod(z + d * pb) * 2 + core)
    src_z = zmod(z - d * pb)
    src_dev = (pb, y_hi * 16 + src_z * 2 + core)
    goal_pb, goal_hi = column(y_hi * 8 + src_z)
    goal_dev = (goal_pb, goal_hi * 16 + zc)
    mine = 2 * pb + y_hi
    from_hi, from_z = mine // 8, mine % 8
    from_pb = zmod(d * (z - from_z))
    from_dev = (from_pb, from_hi * 16 + zc)
    relays_self = pb == 0
    goal_self = jnp.logical_and(goal_pb == pb, goal_hi == y_hi)
    from_self = jnp.logical_and(from_pb == pb, from_hi == y_hi)

    def hop(k, src, dst, to):
        return pltpu.make_async_remote_copy(
            src_ref=src, dst_ref=dst, send_sem=hop_sem.at[2 * k], recv_sem=hop_sem.at[2 * k + 1],
            device_id=to, device_id_type=pl.DeviceIdType.MESH,
        )

    def hop_start(k, src, dst, to, is_self):
        @pl.when(jnp.logical_not(is_self))
        def _():
            hop(k, src, dst, to).start()

        @pl.when(is_self)
        def _():
            dst[...] = src[...]

    def hop_recv(k, src, dst, to, is_self):
        @pl.when(jnp.logical_not(is_self))
        def _():
            hop(k, src, dst, to).wait_recv()

    def hop_sent(k, src, dst, to, is_self):
        @pl.when(jnp.logical_not(is_self))
        def _():
            hop(k, src, dst, to).wait_send()

    h1 = (0, h_own, h_rel, relay_dev, relays_self)
    h2 = (1, h_rel, h_in, goal_dev, goal_self)
    h3 = (2, dh_out, dh_rel, from_dev, from_self)
    h4 = (3, dh_rel, dh_in, src_dev, relays_self)
    w3 = (4, hw_out, hw_rel, from_dev, from_self)
    w4 = (5, hw_rel, hw_in, src_dev, relays_self)

    hop_start(*h1)

    q4, q3l, q3s = [], [], []

    def q_pass(hf):
        f = hf * HALF
        await_rows(q2[hf][0], q_all, qz(z - 2 * d, core), f, HALF)
        share(-2, f, HALF)
        q4.append(push(q_all, qz(z - 2 * d, core), z_dev(2 * d), f, HALF))
        q3l.append(push(q_all, qz(z - 2 * d, core), z_dev(d), f, HALF))
        await_rows(q2[hf][1], q_all, qz(z + 2 * d, core), f, HALF)
        share(2, f, HALF)
        q3s.append(push(q_all, qz(z + 2 * d, core), z_dev(-d), f, HALF))

    q_pass(0)
    await_rows(p_from_xr, p_all, slot_of(xr, y))
    n_xr_yl = push(p_all, slot_of(xr, y), to_yl, A, HALF)
    push(p_all, slot_of(xr, y), to_yr, A, HALF, LAST)
    await_rows(p_from_yr, p_all, slot_of(x, yr))
    m_yr_xl = push(p_all, slot_of(x, yr), to_xl, B, HALF)
    push(p_all, slot_of(x, yr), to_xr, B, HALF, LAST)
    q_pass(1)
    await_rows(p_from_xl, p_all, slot_of(xl, y))
    n_xl_yl = push(p_all, slot_of(xl, y), to_yl, A, HALF)
    push(p_all, slot_of(xl, y), to_yr, A, HALF, LAST)
    await_rows(p_from_yl, p_all, slot_of(x, yl))
    m_yl_xl = push(p_all, slot_of(x, yl), to_xl, B, HALF)
    push(p_all, slot_of(x, yl), to_xr, B, HALF, LAST)
    await_rows(q1l, q_all, qz(z - d, core))
    share(-1)
    await_rows(q1s, q_all, qz(z + d, core))
    share(1)
    await_rows(p_from_x2, p_all, slot_of(x2, y))
    push(p_all, slot_of(x2, y), to_y2, A, HALF, LAST)
    push(p_all, slot_of(x2, y), to_yl, A, HALF, LAST)
    push(p_all, slot_of(x2, y), to_yr, A, HALF, LAST)
    await_rows(p_from_y2, p_all, slot_of(x, y2))
    push(p_all, slot_of(x, y2), to_x2, B, HALF, LAST)
    push(p_all, slot_of(x, y2), to_xl, B, HALF, LAST)
    push(p_all, slot_of(x, y2), to_xr, B, HALF, LAST)
    await_rows(n_xr_yl, p_all, slot_of(xr, yr), A, HALF)
    push(p_all, slot_of(xr, yr), to_yl, A, HALF, LAST)
    await_rows(m_yr_xl, p_all, slot_of(xr, yr), B, HALF)
    push(p_all, slot_of(xr, yr), to_xl, B, HALF, LAST)
    await_rows(n_xl_yl, p_all, slot_of(xl, yr), A, HALF)
    push(p_all, slot_of(xl, yr), to_yl, A, HALF, LAST)
    await_rows(m_yl_xl, p_all, slot_of(xr, yl), B, HALF)
    push(p_all, slot_of(xr, yl), to_xl, B, HALF, LAST)
    hop_recv(*h1)
    hop_start(*h2)
    for hf in range(2):
        f = hf * HALF
        await_rows(q3s[hf], q_all, qz(z + 3 * d, core), f, HALF)
        share(3, f, HALF)
        await_rows(q3l[hf], q_all, qz(z - 3 * d, core), f, HALF)
        share(-3, f, HALF)
    for hf in range(2):
        f = hf * HALF
        await_rows(q4[hf], q_all, qz(z + 4, core), f, HALF)
        share(4, f, HALF)

    arrive(LAST, p_all.at[pl.ds(0, 14 * HALF)])

    csum[...] = jnp.zeros_like(csum)

    def score(t, carry):
        first = pl.multiple_of(t * TILE, TILE)
        s = nt(q_all[pl.ds(first, TILE), :], p_all[...])
        e = jnp.exp(inverse_temp * s - inverse_temp)
        e_s[pl.ds(first, TILE), :] = e
        csum[...] += jnp.sum(e.reshape(TILE // 8, 8, GROUP), axis=0)
        part = e[:, :128]
        for j in range(1, GROUP // 128):
            part = part + e[:, j * 128 : (j + 1) * 128]
        for j in range(TILE // 128):
            row = jnp.sum(jnp.transpose(part[j * 128 : (j + 1) * 128, :]), axis=0, keepdims=True)
            tq[q_slot, pl.ds(t * (TILE // 128) + j, 1), :] = row
        return carry

    for i in range(2):
        score(core * 2 + i, 0)
    arrive(SHARED, q_all.at[pl.ds(0, 8 * ROWS)])
    for i in range(2):
        score((1 - core) * 2 + i, 0)
    total = jnp.sum(csum[...], axis=0, keepdims=True)
    for j in range(GROUP // 128):
        tp[p_slot, pl.ds(j, 1), :] = total[:, j * 128 : (j + 1) * 128]

    def total_copies(k, count):
        first_q, first_p = (q_slot, p_slot) if count == 1 else (0, 0)
        return [
            pltpu.make_async_remote_copy(
                src_ref=ref.at[pl.ds(first, count)], dst_ref=ref.at[pl.ds(first, count)],
                send_sem=t_sem.at[2 * i], recv_sem=t_sem.at[2 * i + 1], device_id=to, device_id_type=pl.DeviceIdType.MESH,
            )
            for i, (ref, first, to) in enumerate(
                ((tq, first_q, q_peer((q_slot + k) % 16)), (tp, first_p, p_peer((p_slot + k) % 16)))
            )
        ]

    for k in (10, 9, 11, 6, 14, 2, 8, 5, 7, 13, 15, 1, 3, 4, 12):
        total_copies(k, 1)[1].start()

    hop_recv(*h2)

    def block_rows(j):
        return pl.ds(pl.multiple_of((j // 2) * 512 + core * 256 + (j % 2) * 128, 128), 128)

    q_half = jnp.concatenate([q_all[block_rows(j), :] for j in range(4)], axis=0)
    idx_copy.wait()
    hidx = idx_s[y_hi * 2 + core] - (from_hi * 16 + q_slot_of(from_z)) * 512 - from_pb * ROWS
    hidx = jnp.concatenate(
        [hidx[j : j + 1, c * ROWS : (c + 1) * ROWS] for c in range(2) for j in range(4)], axis=1
    )
    named = lax.broadcasted_iota(jnp.int32, (ROWS, 512), 0) == hidx
    e_hard = jnp.exp(inverse_temp * nt(h_in[...], q_half) - inverse_temp)
    e_hard = jnp.where(named, e_hard, 0.0)
    eh[...] = e_hard
    hard_sum = jnp.sum(e_hard, axis=0, keepdims=True)
    for j in range(4):
        tq[q_slot, pl.ds((j // 2) * 4 + core * 2 + j % 2, 1), :] += hard_sum[:, j * 128 : (j + 1) * 128]

    eye = lax.broadcasted_iota(jnp.int32, (128, 128), 0) == lax.broadcasted_iota(jnp.int32, (128, 128), 1)

    for k in (4, 12, 5, 3, 11, 13, 6, 2, 10, 14, 7, 1, 9, 15, 8):
        total_copies(k, 1)[0].start()

    dh_out[...] = jnp.dot(named.astype(bf16), q_half, preferred_element_type=f32).astype(bf16)
    hop_start(*h3)

    is_keeper = z == mine % 8
    kb = mine // 8
    ka = core

    @pl.when(is_keeper)
    def _():
        for j in range(4):
            q_rows = q_all[block_rows(j), :]
            p_rows = p_all[pl.ds(pl.multiple_of(kb * 512 + j * 128, 128), 128), :]
            diag = jnp.where(eye, inverse_temp * nt(q_rows, p_rows), 0.0)
            dg[j : j + 1, :] = jnp.sum(diag, axis=0, keepdims=True)

    def diag_copy(k, dst, to, at):
        return pltpu.make_async_remote_copy(
            src_ref=dg, dst_ref=dst, send_sem=dg_send.at[k], recv_sem=dg_recv.at[at],
            device_id=to, device_id_type=pl.DeviceIdType.MESH,
        )

    def keep(act):
        @pl.when(is_keeper)
        def _():
            for k in range(8):
                sq, sp = (k // 4) * 8 + ka * 4 + k % 4, kb * 8 + k

                @pl.when(sq != q_slot)
                def _():
                    act(diag_copy(k, dgq, q_peer(sq), 0))

                @pl.when(sp != p_slot)
                def _():
                    act(diag_copy(8 + k, dgp, p_peer(sp), 1))

    keep(lambda copy: copy.start())
    dgq_self = jnp.logical_and(is_keeper, z // 4 == ka)
    dgp_self = jnp.logical_and(is_keeper, p_slot // 8 == kb)

    @pl.when(dgq_self)
    def _():
        dgq[...] = dg[...]

    @pl.when(dgp_self)
    def _():
        dgp[...] = dg[...]

    def turn(k, carry):
        first = pl.multiple_of(k * CHUNK, CHUNK)
        wt[:, pl.ds(first, CHUNK)] = jnp.transpose(w[pl.ds(first, CHUNK), :])
        return carry

    lax.fori_loop(0, MODEL // CHUNK, turn, 0)
    all_sent(0)
    for copy in total_copies(1, 15):
        copy.wait()
    sq = jnp.sum(tq[...], axis=0)
    sp = jnp.sum(tp[...], axis=0)
    rinv = inverse_temp / sq
    cinv = inverse_temp / sp
    rin_s[...] = rinv
    lrow_s[0:8, :] = sq
    lrow_s[8:16, :] = sp

    hard_weight = jnp.concatenate([rin_s[pl.ds((j // 2) * 4 + core * 2 + j % 2, 1), :] for j in range(4)], axis=1)
    weighted = eh[...] * hard_weight
    gh[...] = weighted.astype(bf16)
    hw_out[...] = jnp.broadcast_to(jnp.sum(weighted, axis=1, keepdims=True), (ROWS, 128))
    hop_start(*w3)
    for j in range(8):
        rcol[j * 128 : (j + 1) * 128, :] = jnp.transpose(jnp.broadcast_to(rinv[j : j + 1, :], (128, 128)))
        crow[:, j * 128 : (j + 1) * 128] = jnp.broadcast_to(cinv[j : j + 1, :], (8, 128))
    tile_s[...] = tn(gh[...], h_in[...])

    @pl.when(is_keeper)
    def _():
        for j in range(4):
            r = block_rows(j)
            c = pl.multiple_of(kb * 512 + j * 128, 128)
            factor = rcol[r, :] + crow[0:1, pl.ds(c, 128)]
            e_s[r, pl.ds(c, 128)] -= jnp.where(eye, 2.0 * inverse_temp / factor, 0.0)

    def question_tile(t):
        first = pl.multiple_of(t * TILE, TILE)
        factor = wide(rcol[pl.ds(first, TILE), :], GROUP // 128) + crow[0:1, :]
        weights = (e_s[pl.ds(first, TILE), :] * factor).astype(bf16)
        g_s[pl.ds(first, TILE), :] = weights
        value = jnp.dot(weights, p_all[...], preferred_element_type=f32)
        here = (t % 2 == core).astype(f32)
        value = value + here * tile_s[pl.ds(pl.multiple_of((t // 2) * TILE, TILE), TILE), :]
        for j in range(4):
            dq[t // 2, (t % 2) * 4 + j] = value[j * ROWS : (j + 1) * ROWS, :].astype(bf16)

    def four(ref, i):
        return ref.at[pl.ds(i * 4, 4)]

    phase[0] = 1
    n_pt = []
    for i in range(2):
        question_tile((1 - core) * 2 + i)
        n_pt.append(remote(four(dq.at[1 - core], i), four(prt, i), other))
    hop_recv(*h3)
    hop_start(*h4)
    for i in range(2):
        question_tile(core * 2 + i)

    def passage_tile(yy):
        first = pl.multiple_of(yy * TILE, TILE)
        value = tn(g_s[:, pl.ds(first, TILE)], q_all[...]).astype(bf16)
        for j in range(4):
            dpa[yy, j] = value[j * ROWS : j * ROWS + HALF, :]
            dpb[j, yy] = value[j * ROWS + HALF : (j + 1) * ROWS, :]

    def pair(ref, i):
        return ref.at[pl.ds(i * 2, 2)]

    def half(ref, hf):
        return ref.at[pl.ds(hf * HALF, HALF)]

    n_b1, n_b1s = [], []

    def send_b(yy):
        n_b1.append(remote(dpb.at[x2, yy], b1.at[0, yy], to_xr))
        n_b1s.append(remote(dpb.at[xl, yy], b1.at[1, yy], to_xl))

    passage_tile(y2)
    n_a1 = [remote(pair(dpa.at[y2], i), pair(a1.at[0], i), to_yr) for i in range(2)]
    send_b(y2)
    for i in range(2):
        arrive(n_pt[i], four(prt, i))
        prt[i * 4 : i * 4 + 4] = (
            prt[i * 4 : i * 4 + 4].astype(f32) + dq[core, i * 4 : i * 4 + 4].astype(f32)
        ).astype(bf16)
    r4, r3l, r3s = [], [], []
    for hf in range(2):
        r4.append(remote(half(prt.at[zmod(z + 4)], hf), half(zr.at[0], hf), z_dev(-2 * d)))
        r3l.append(remote(half(prt.at[zmod(z - 3 * d)], hf), half(zr.at[1], hf), z_dev(-d)))
        r3s.append(remote(half(prt.at[zmod(z + 3 * d)], hf), half(zr.at[2], hf), z_dev(d)))
    r1l = remote(prt.at[zmod(z - d)], zin.at[0], z_dev(-d))
    r1s = remote(prt.at[zmod(z + d)], zin.at[1], z_dev(d))
    passage_tile(yl)
    n_a1s = remote(dpa.at[yl], a1.at[1], to_yl)
    send_b(yl)
    passage_tile(yr)
    send_b(yr)
    passage_tile(y)
    send_b(y)

    n_a1l, n_b1l = [], []
    for i in range(2):
        two = slice(i * 2, i * 2 + 2)
        arrive(n_a1[i], pair(a1.at[0], i))
        a1[0, two] = (a1[0, two].astype(f32) + dpa[yr, two].astype(f32)).astype(bf16)
        n_a1l.append(remote(pair(a1.at[0], i), pair(a1.at[2], i), to_yr))

    r2l, r2s = [], []
    def q_relay(hf):
        part = slice(hf * HALF, (hf + 1) * HALF)
        arrive(r3s[hf], half(zr.at[2], hf))
        zr[2, part, :] = (zr[2, part, :].astype(f32) + prt[zmod(z + 2 * d), part, :].astype(f32)).astype(bf16)
        r2s.append(remote(half(zr.at[2], hf), half(zin.at[3], hf), z_dev(2 * d)))
        arrive(r3l[hf], half(zr.at[1], hf))
        arrive(r4[hf], half(zr.at[0], hf))
        zr[1, part, :] = (
            zr[1, part, :].astype(f32) + zr[0, part, :].astype(f32) + prt[zmod(z - 2 * d), part, :].astype(f32)
        ).astype(bf16)
        r2l.append(remote(half(zr.at[1], hf), half(zin.at[2], hf), z_dev(-2 * d)))

    def b_relay(i, yy):
        arrive(n_b1[i], b1.at[0, yy])
        b1[0, yy] = (b1[0, yy].astype(f32) + dpb[xr, yy].astype(f32)).astype(bf16)
        n_b1l.append(remote(b1.at[0, yy], b1.at[2, yy], to_xr))

    b_relay(0, y2)
    b_relay(1, yl)
    q_relay(0)
    b_relay(2, yr)
    b_relay(3, y)
    q_relay(1)

    hop_recv(*w3)
    hop_start(*w4)

    arrive(n_a1s, a1.at[1])
    for i in range(2):
        arrive(n_a1l[i], pair(a1.at[2], i))
    a1[1] = (a1[1].astype(f32) + a1[2].astype(f32) + dpa[y].astype(f32)).astype(bf16)
    n_a2 = [remote(a1.at[1, xx], a2.at[i], to) for i, (xx, to) in enumerate(((x2, to_x2), (xl, to_xl), (xr, to_xr)))]
    for i, yy in enumerate((y2, yl, yr, y)):
        arrive(n_b1s[i], b1.at[1, yy])
        arrive(n_b1l[i], b1.at[2, yy])
    b1[1] = (b1[1].astype(f32) + b1[2].astype(f32) + dpb[x].astype(f32)).astype(bf16)
    n_b2 = [remote(b1.at[1, yy], b2.at[i], to) for i, (yy, to) in enumerate(((y2, to_y2), (yl, to_yl), (yr, to_yr)))]

    def back(grad, i, first, count):
        part = slice(i * ROWS + first, i * ROWS + first + count)
        u = unit[part, :]
        along = jnp.sum(grad * u, axis=1, keepdims=True)
        ge[part, :] = ((grad - u * along) * wide(scale[part, :], WIDTH // 128)).astype(bf16)

    keeper_q = mine % 8
    group_p = y_hi * 8 + z

    @pl.when(jnp.logical_not(dgq_self))
    def _():
        diag_copy(0, dgq, (pb, y_hi * 16 + keeper_q * 2 + z // 4), 0).wait_recv()

    @pl.when(jnp.logical_not(dgp_self))
    def _():
        diag_copy(0, dgp, (group_p // 2, (group_p % 2) * 16 + zc), 1).wait_recv()

    def loss(total_row, diag, first):
        value = inverse_temp + jnp.log(total_row) - diag
        return jnp.where(first, value[:, :ROWS], value[:, ROWS:])

    loss_s[0, 0:1, 0:ROWS] = loss(lrow_s[pl.ds(core * 4 + z // 2, 1), :], dgq[pl.ds(core * 2 + (z % 4) // 2, 1), :], z % 2 == 0)
    loss_s[1, 0:1, 0:ROWS] = loss(lrow_s[pl.ds(8 + y * 2 + x // 2, 1), :], dgp[pl.ds(y_lo * 2 + x // 2, 1), :], x % 2 == 0)
    loss_copies = [pltpu.make_async_copy(loss_s.at[i], ref, o_sem.at[3, i]) for i, ref in enumerate((lq_ref, lp_ref))]
    for copy in loss_copies:
        copy.start()

    hop_recv(*h4)
    hop_recv(*w4)
    grad_h = (dh_in[...].astype(f32) * wide(hw_in[...], WIDTH // 128)).astype(bf16)
    back(grad_h.astype(f32), 2, 0, ROWS)

    arrive(r1l, zin.at[0])
    arrive(r1s, zin.at[1])
    for hf in range(2):
        arrive(r2s[hf], half(zin.at[3], hf))
        arrive(r2l[hf], half(zin.at[2], hf))
    back(jnp.sum(zin[...].astype(f32), axis=0) + prt[z].astype(f32), 0, 0, ROWS)
    for i in range(3):
        arrive(n_a2[i], a2.at[i])
    back(jnp.sum(a2[...].astype(f32), axis=0) + a1[1, x].astype(f32), 1, 0, HALF)
    for i in range(3):
        arrive(n_b2[i], b2.at[i])
    back(jnp.sum(b2[...].astype(f32), axis=0) + b1[1, y].astype(f32), 1, HALF, HALF)

    def out_copies(k):
        columns = pl.ds(pl.multiple_of(k * CHUNK, CHUNK), CHUNK)
        return [
            pltpu.make_async_copy(out_s.at[pl.ds(i * ROWS, ROWS), columns], ref.at[:, columns], o_sem.at[i, k])
            for i, ref in enumerate((oq_ref, op_ref, oh_ref))
        ]

    def unproject(k, carry):
        first = pl.multiple_of(k * CHUNK, CHUNK)
        out_s[:, pl.ds(first, CHUNK)] = jnp.dot(
            ge[...], wt[:, pl.ds(first, CHUNK)], preferred_element_type=f32
        ).astype(bf16)
        for copy in out_copies(k):
            copy.start()
        return carry

    for k in range(MODEL // CHUNK):
        unproject(k, 0)

    all_sent(1)
    for h in (h1, h2, h3, h4, w3, w4):
        hop_sent(*h)
    keep(lambda copy: copy.wait_send())
    for k in range(MODEL // CHUNK):
        for copy in out_copies(k):
            copy.wait()
    for copy in loss_copies:
        copy.wait()


def hand_on(gq, gp, gh, lq, lp, oq, op, oh, olq, olp, stage, lstage, lflat, in_sem, out_sem):
    arrivals = [pltpu.make_async_copy(src, stage.at[i], in_sem.at[i]) for i, src in enumerate((gq, gp, gh))]
    losses = [pltpu.make_async_copy(src, lstage.at[i], in_sem.at[3 + i]) for i, src in enumerate((lq, lp))]
    leaving = [pltpu.make_async_copy(stage.at[i], dst, out_sem.at[i]) for i, dst in enumerate((oq, op, oh))]
    leaving += [pltpu.make_async_copy(lflat.at[i], dst, out_sem.at[3 + i]) for i, dst in enumerate((olq, olp))]
    for copy in losses + arrivals:
        copy.start()
    for i, copy in enumerate(losses):
        copy.wait()
        lflat[i, :] = lstage[i, 0, 0:ROWS]
        leaving[3 + i].start()
    for i, copy in enumerate(arrivals):
        copy.wait()
        leaving[i].start()
    for copy in leaving:
        copy.wait()


COPIES = 130


def shards(questions, passages, hard_rows, hard_index, projection):
    vmem = pl.BlockSpec(memory_space=pltpu.VMEM)
    hbm = pl.BlockSpec(memory_space=pl.ANY)
    out = jax.ShapeDtypeStruct((ROWS, MODEL), bf16)
    loss = jax.ShapeDtypeStruct((8, 128), f32)
    flat = jax.ShapeDtypeStruct((ROWS,), f32)
    V, D = pltpu.VMEM, pltpu.SemaphoreType.DMA
    gq, gp, gh, lq, lp = pl.pallas_call(
        kernel,
        out_shape=(out, out, out, loss, loss),
        in_specs=[hbm] * 5,
        out_specs=(hbm,) * 5,
        scratch_shapes=[
            V((3 * ROWS, MODEL), bf16),
            V((MODEL, WIDTH), bf16),
            V((WIDTH, MODEL), bf16),
            V((3 * ROWS, WIDTH), f32),
            V((3 * ROWS, WIDTH), f32),
            V((3 * ROWS, 128), f32),
            V((GROUP, WIDTH), bf16),
            V((GROUP, WIDTH), bf16),
            V((ROWS, WIDTH), bf16),
            V((ROWS, WIDTH), bf16),
            V((ROWS, WIDTH), bf16),
            V((ROWS, WIDTH), bf16),
            V((ROWS, WIDTH), bf16),
            V((ROWS, WIDTH), bf16),
            V((ROWS, 128), f32),
            V((ROWS, 128), f32),
            V((ROWS, 128), f32),
            V((ROWS, 512), f32),
            V((ROWS, 512), bf16),
            V((GROUP, GROUP), f32),
            V((GROUP, GROUP), bf16),
            V((512, WIDTH), f32),
            V((8, GROUP), f32),
            V((16, 8, 128), f32),
            V((16, 8, 128), f32),
            V((GROUP, 128), f32),
            V((8, GROUP), f32),
            V((8, 128), f32),
            V((8, 128), f32),
            V((8, 128), f32),
            V((8, 128), f32),
            V((16, 128), f32),
            V((2, 8, ROWS, WIDTH), bf16),
            V((8, ROWS, WIDTH), bf16),
            V((3, ROWS, WIDTH), bf16),
            V((4, ROWS, WIDTH), bf16),
            V((4, 4, HALF, WIDTH), bf16),
            V((4, 4, HALF, WIDTH), bf16),
            V((3, 4, HALF, WIDTH), bf16),
            V((3, 4, HALF, WIDTH), bf16),
            V((3, HALF, WIDTH), bf16),
            V((3, HALF, WIDTH), bf16),
            V((3 * ROWS, WIDTH), bf16),
            V((3 * ROWS, MODEL), bf16),
            V((4, 4, 128), jnp.int32),
            V((2, 8, 128), f32),
            D((4,)), D((MODEL // CHUNK,)),
            D((2,)), D((COPIES,)),
            D((4,)),
            D((16,)), D((2,)), D((12,)), D((4, MODEL // CHUNK)),
        ],
        compiler_params=pltpu.CompilerParams(
            collective_id=0, has_side_effects=True, vmem_limit_bytes=56 * 1024 * 1024
        ),
        cost_estimate=pl.CostEstimate(flops=8 * 10**9, bytes_accessed=10**7, transcendentals=10**6),
    )(questions, passages, hard_rows, hard_index.reshape(4, 4, 128), projection)
    return pl.pallas_call(
        hand_on,
        out_shape=(out, out, out, flat, flat),
        in_specs=(hbm,) * 5,
        out_specs=(hbm,) * 5,
        scratch_shapes=[V((3, ROWS, MODEL), bf16), V((2, 8, 128), f32), V((2, ROWS), f32), D((5,)), D((5,))],
        compiler_params=pltpu.CompilerParams(vmem_limit_bytes=56 * 1024 * 1024),
        cost_estimate=pl.CostEstimate(flops=0, bytes_accessed=3 * 10**6, transcendentals=0),
    )(gq, gp, gh, lq, lp)


def solution(mesh):
    in_specs = (P(("pb", "pa"), None), P(("pa", "pb"), None), P(("pa", "pb"), None), P("pb"), P())
    out_specs = (
        P(("pb", "pa"), None),
        P(("pa", "pb"), None),
        P(("pa", "pb"), None),
        P(("pb", "pa")),
        P(("pa", "pb")),
    )
    return jax.shard_map(shards, mesh=mesh, in_specs=in_specs, out_specs=out_specs, check_vma=False)
```
